512 devices in a mesh: seq: 128 (over y, x, z_lo), ch: 4 (over z_hi, core).
Axes of the slice: x: 4, y: 8, z: 8 (z_hi: 2, z_lo: 4; z = z_hi * 4 + z_lo), core: 2. Of those that a mesh axis runs over, the one named last changes fastest.
Arguments:
- bases: int32 [49152], P('seq'), may hold values from 0 to 3
- conv1_weight: bfloat16 [4, 15, 768], P(None, None, 'ch'), may hold values from -0.75 to 0.75
- gain1: float32 [768], P('ch'), may hold values from 0.5 to 1.5
- conv2_weight: bfloat16 [768, 5, 1024], P(None, None, 'ch'), may hold values from -0.09375 to 0.09375
- gain2: float32 [1024], P('ch'), may hold values from 0.5 to 1.5
- cotangent: bfloat16 [49152, 1024], P('seq', 'ch'), may hold values from -0.02734375 to 0.02734375
Outputs:
- features: bfloat16 [49152, 1024], P('seq', 'ch')
- grad_w1: float32 [4, 15, 768], P(None, None, 'ch')
- grad_gain1: float32 [768], P('ch')
- grad_w2: float32 [768, 5, 1024], P('seq', None, 'ch')
- grad_gain2: float32 [1024], P('ch')
The draws below stay inside these ranges and needn't reach their ends.
All inputs are finite; a program needn't handle non-finite values.
Results may differ from the reference program's by a relative error of at most 0.019.
Values may be sent and summed in bfloat16 or wider, within the bound.
A program may use at most 64 MiB of HBM per device.

```python
import jax
import jax.numpy as jnp
from jax import lax

BASES = 4
KW1 = 15
KW2 = 5
D1 = 768
D2 = 1024
POSITIONS = 49152
N_CH = 4


def touch_ends(entries, rng, low, top_value):
    longest = entries.shape.index(max(entries.shape))
    spots = []
    for shift in (0, 1):
        where = [jax.random.randint(jax.random.fold_in(rng, axis), (), 0, length) for axis, length in enumerate(entries.shape)]
        where[longest] = (where[longest] + shift) % entries.shape[longest]
        spots.append(tuple(where))
    return entries.at[spots[0]].set(low).at[spots[1]].set(top_value)


def level_of(key, extent, split, least, largest):
    loudness, own = 1.0, jax.random.fold_in(key, 6)
    for position, shards_of in split:
        heights = jnp.exp(jax.random.uniform(jax.random.fold_in(own, position), (shards_of,), jnp.float32, least / len(split), largest / len(split)))
        loudness = loudness * jnp.repeat(heights, extent[position] // shards_of).reshape([-1 if axis == position else 1 for axis in range(len(extent))])
    return loudness


def bell_draw(rng, shape, width, most, split=(), kind=jnp.bfloat16):
    gain = level_of(rng, shape, split, -0.22, 0.18) if split else 1.0
    drawn = jax.random.normal(rng, shape, jnp.float32) * width * gain
    return jnp.minimum(jnp.maximum(drawn, -most), most).astype(kind)


def setup_inputs(seed: int = 0) -> dict:
    key_of = jax.random.split(jax.random.key(seed), 7)
    bases = touch_ends(jax.random.randint(key_of[0], (POSITIONS,), 0, 4), jax.random.fold_in(key_of[0], 1), 0, 3).astype(jnp.int32)
    conv1_weight = bell_draw(key_of[1], (BASES, KW1, D1), (BASES * KW1) ** -0.5, 0.75, ((2, 4),))
    gain1 = jnp.clip(1.0 + 0.1 * jax.random.normal(key_of[2], (D1,), jnp.float32), 0.5, 1.5)
    conv2_weight = bell_draw(key_of[3], (D1, KW2, D2), (D1 * KW2) ** -0.5, 0.09375, ((2, 4),))
    gain2 = jnp.clip(1.0 + 0.1 * jax.random.normal(key_of[4], (D2,), jnp.float32), 0.5, 1.5)
    cotangent = bell_draw(key_of[5], (POSITIONS, D2), (1.0 / POSITIONS ** 0.5), 0.02734375, ((0, 128), (1, 4)))
    return {"bases": bases, "conv1_weight": conv1_weight, "gain1": gain1, "conv2_weight": conv2_weight, "gain2": gain2, "cotangent": cotangent}


epsilon = 1e-06

def convolve(inputs, kernel, taps):
    rim = taps // 2
    length = inputs.shape[0]
    padded = jnp.pad(inputs, ((rim, rim), (0, 0)))
    total = jnp.zeros((length, kernel.shape[2]), jnp.float32)
    for tap in range(taps):
        total = total + jnp.dot(padded[tap:tap + length], kernel[:, tap, :], preferred_element_type=jnp.float32)
    return (total, padded)

def kernel_grad(padded, grads, taps):
    length = grads.shape[0]
    rows = []
    for tap in range(taps):
        rows.append(lax.dot_general(padded[tap:tap + length], grads, (((0,), (0,)), ((), ())), preferred_element_type=jnp.float32))
    return jnp.stack(rows, axis=1)

def reference(bases, conv1_weight, gain1, conv2_weight, gain2, cotangent):
    length = bases.shape[0]
    onehot = (bases[:, None] == jnp.arange(BASES, dtype=jnp.int32)[None, :]).astype(jnp.bfloat16)
    conv1, onehot_pad = convolve(onehot, conv1_weight, KW1)
    scale1 = lax.rsqrt(lax.optimization_barrier(jnp.mean(conv1 * conv1, axis=1)) + epsilon)
    normed1 = conv1 * scale1[:, None]
    pre1 = normed1 * gain1
    act1 = jax.nn.gelu(pre1).astype(jnp.bfloat16)
    conv2, act_pad = convolve(act1, conv2_weight, KW2)
    scale2 = lax.rsqrt(lax.optimization_barrier(jnp.mean(conv2 * conv2, axis=1)) + epsilon)
    normed2 = conv2 * scale2[:, None]
    pre2 = normed2 * gain2
    features = jax.nn.gelu(pre2).astype(jnp.bfloat16)
    _, pull2 = jax.vjp(jax.nn.gelu, pre2)
    dpre2 = pull2(cotangent.astype(jnp.float32))[0]
    grad_gain2 = lax.optimization_barrier(jnp.sum(dpre2 * normed2, axis=0))
    dnormed2 = dpre2 * gain2
    mean2 = lax.optimization_barrier(jnp.mean(dnormed2 * normed2, axis=1))
    dconv2 = (scale2[:, None] * (dnormed2 - normed2 * mean2[:, None])).astype(jnp.bfloat16)
    grad_w2 = kernel_grad(act_pad, dconv2, KW2)
    rim2 = KW2 // 2
    grad_pad = jnp.pad(dconv2, ((rim2, rim2), (0, 0)))
    group = D2 // N_CH
    dact1 = jnp.zeros((length, D1), jnp.float32)
    for index in range(N_CH):
        part = jnp.zeros((length, D1), jnp.float32)
        for tap in range(KW2):
            start = 2 * rim2 - tap
            part = part + lax.dot_general(grad_pad[start:start + length, index * group:(index + 1) * group], conv2_weight[:, tap, index * group:(index + 1) * group], (((1,), (1,)), ((), ())), preferred_element_type=jnp.float32)
        dact1 = dact1 + lax.optimization_barrier(part.astype(jnp.bfloat16)).astype(jnp.float32)
    _, pull1 = jax.vjp(jax.nn.gelu, pre1)
    dpre1 = pull1(dact1)[0]
    grad_gain1 = lax.optimization_barrier(jnp.sum(dpre1 * normed1, axis=0))
    dnormed1 = dpre1 * gain1
    mean1 = lax.optimization_barrier(jnp.mean(dnormed1 * normed1, axis=1))
    dconv1 = (scale1[:, None] * (dnormed1 - normed1 * mean1[:, None])).astype(jnp.bfloat16)
    grad_w1 = kernel_grad(onehot_pad, dconv1, KW1)
    return (features, grad_w1, grad_gain1, grad_w2, grad_gain2)
```

```python
import math

import jax
import jax.numpy as jnp
from jax import lax
from jax.experimental import pallas as pl
from jax.experimental.pallas import tpu as pltpu
from jax.sharding import PartitionSpec as P

BASES = 4
KW1 = 15
KW2 = 5
D1 = 768
D2 = 1024
OWN1 = 192
OWN2 = 256
ROWS = 384
FRAME = 416
NX, NY, NZ, NC = 4, 8, 4, 4
NS = NX * NY * NZ
PART = ROWS // NC
CHUNK = 240
RA = 80
RB = CHUNK - RA
EPS = 1e-06
MESH = pl.DeviceIdType.MESH
F32 = jnp.float32
BF16 = jnp.bfloat16
ROOT = math.sqrt(2.0 / math.pi)

S_BASE, S_COT, S_W1, S_G1 = 0, 2, 4, 7
S_SQ, S_IN = 10, 13
S_CORE, S_ZHI, S_CH = 16, 18, 19
S_AY, S_BX, S_AX, S_BY, S_Z = 22, 29, 32, 35, 42
S_RX, S_RY, S_RZ = 45, 48, 55
N_SEM = 58


def gelu_parts(v):
    square = v * v
    t = jnp.tanh(ROOT * (v + 0.044715 * (square * v)))
    cdf = 0.5 * (1.0 + t)
    slope = cdf + (0.5 * ROOT) * v * (1.0 - t * t) * (1.0 + (3.0 * 0.044715) * square)
    return cdf, slope


def nt_dot(a, b):
    return lax.dot_general(a, b, (((1,), (1,)), ((), ())), preferred_element_type=F32)


def tn_dot(a, b):
    return lax.dot_general(a, b, (((0,), (0,)), ((), ())), preferred_element_type=F32)


def kernel(
    bases_ref, w1_ref, g1_ref, w2_ref, g2_ref, cot_ref,
    feat_ref, gw1_ref, gg1_ref, gw2_ref, gg2_ref,
    bext, cext, w1g, g1g, gain1, w1full, ut, uu, n1, s1, act, actt,
    w2v, ybuf, c2, dn2, q, s2, m2, sqs, ins, d2, dcat, g2acc, g1acc,
    pb, pcin, zs_, zr_, dc1, pay, chs, chr_, axs, ays, azs,
    big, rya, rxb, a2, b2, rxa, ryb, fin, zsl, rzl,
    ssem, rsem, lsem,
):
    s = lax.axis_index("seq")
    c = lax.axis_index("ch")
    z = lax.rem(s, NZ)
    x = lax.rem(lax.div(s, NZ), NX)
    y = lax.div(s, NZ * NX)
    core = lax.rem(c, 2)
    zh = lax.div(c, 2)

    def seq_of(yy, xx, zz):
        return (yy * NX + xx) * NZ + zz

    def x_peer(k):
        return lax.rem(x + k, NX)

    def y_peer(k):
        return lax.rem(y + k, NY)

    def z_peer(k):
        return lax.rem(z + k, NZ)

    def c_peer(k):
        return lax.rem(c + k, NC)

    right = lax.rem(s + 1, NS)
    left = lax.rem(s + NS - 1, NS)

    load_w2 = pltpu.make_async_copy(w2_ref, w2v, lsem.at[0])
    load_w2.start()
    load_cot = pltpu.make_async_copy(cot_ref, cext.at[pl.ds(16, ROWS)], lsem.at[1])
    load_cot.start()

    barrier = pltpu.get_barrier_semaphore()
    friends = [(right, c), (left, c)]
    friends += [(s, c_peer(k)) for k in range(1, NC)]
    friends += [(seq_of(y, x_peer(k), z), c) for k in range(1, NX)]
    friends += [(seq_of(y_peer(k), x, z), c) for k in range(1, NY)]
    friends += [(seq_of(y, x, z_peer(k)), c) for k in range(1, NZ)]
    for friend in friends:
        pl.semaphore_signal(barrier, inc=1, device_id=friend, device_id_type=MESH)
    pl.semaphore_wait(barrier, len(friends))

    pending = []

    def send(src, dst, number, to):
        copy = pltpu.make_async_remote_copy(
            src_ref=src,
            dst_ref=dst,
            send_sem=ssem.at[number],
            recv_sem=rsem.at[number],
            device_id=to,
            device_id_type=MESH,
        )
        copy.start()
        pending.append(copy)
        return copy

    def arrived(copies):
        for copy in copies:
            copy.wait_recv()

    got_bases = [
        send(bases_ref.at[:, pl.ds(256, 128)], bext.at[:, pl.ds(0, 128)], S_BASE, (right, c)),
        send(bases_ref.at[:, pl.ds(0, 128)], bext.at[:, pl.ds(512, 128)], S_BASE + 1, (left, c)),
    ]
    got_w1 = []
    for k in range(1, NC):
        to = (s, c_peer(k))
        got_w1.append(send(w1_ref, w1g.at[c], S_W1 + k - 1, to))
        got_w1.append(send(g1_ref, g1g.at[c], S_G1 + k - 1, to))
    got_cot = [
        send(cot_ref.at[pl.ds(ROWS - 16, 16)], cext.at[pl.ds(0, 16)], S_COT, (right, c)),
        send(cot_ref.at[pl.ds(0, 16)], cext.at[pl.ds(16 + ROWS, 16)], S_COT + 1, (left, c)),
    ]
    bext[:, pl.ds(128, ROWS)] = bases_ref[...]
    w1g[c] = w1_ref[...]
    g1g[c] = g1_ref[...]

    arrived(got_bases)
    place = lax.broadcasted_iota(jnp.int32, (1, 640), 1) - 128 + s * ROWS
    known = jnp.where((place >= 0) & (place < NS * ROWS), bext[...], -1)
    kinds = lax.broadcasted_iota(jnp.int32, (BASES, 512), 0)
    for tap in range(KW1):
        rolled = pltpu.roll(known, 640 - (105 + tap), 1)[:, :512]
        ut[pl.ds(BASES * tap, BASES), :] = (
            jnp.broadcast_to(rolled, (BASES, 512)) == kinds
        ).astype(F32)
    ut[pl.ds(BASES * KW1, 4), :] = jnp.zeros((4, 512), F32)
    for block in range(4):
        uu[pl.ds(128 * block, 128), :] = ut[:, pl.ds(128 * block, 128)].T.astype(BF16)

    arrived(got_w1)
    w1full[...] = jnp.concatenate(
        [w1g[k][:, :OWN1].astype(F32) for k in range(NC)], axis=1
    ).astype(BF16)
    gain1[...] = jnp.concatenate([g1g[k][:, :OWN1] for k in range(NC)], axis=1)
    n1[...] = jnp.dot(uu[pl.ds(0, FRAME), :], w1full[...], preferred_element_type=F32)

    @pl.loop(0, FRAME // 32)
    def _(i):
        rows = pl.ds(pl.multiple_of(i * 32, 32), 32)
        v = n1[rows, :]
        scale = lax.rsqrt(jnp.sum(v * v, axis=1, keepdims=True) * (1.0 / D1) + EPS)
        normed = v * scale
        n1[rows, :] = normed
        s1[rows, :] = jnp.broadcast_to(scale, (32, 128))
        pre = normed * gain1[...]
        cdf, _ = gelu_parts(pre)
        where = lax.broadcasted_iota(jnp.int32, (32, 1), 0) + (i * 32 - 16) + s * ROWS
        inside = (where >= 0) & (where < NS * ROWS)
        act[rows, :] = jnp.where(inside, pre * cdf, 0.0).astype(BF16)

    load_w2.wait()

    @pl.loop(0, KW2)
    def _(tap):
        ybuf[tap] = jnp.dot(act[...], w2v[tap], preferred_element_type=F32)

    pieces = [(8, 8)] + [(16 + 48 * k, 48) for k in range(8)] + [(400, 8)]
    q[pl.ds(0, 8), :] = jnp.zeros((8, 128), F32)
    q[pl.ds(408, 104), :] = jnp.zeros((104, 128), F32)
    for start, count in pieces:
        total = ybuf[0, pl.ds(start - 2, count), :]
        for tap in range(1, KW2):
            total = total + ybuf[tap, pl.ds(start + tap - 2, count), :]
        c2[pl.ds(start, count), :] = total
        lo, hi = total[:, :128], total[:, 128:]
        q[pl.ds(start, count), :] = lo * lo + hi * hi

    def row_sums(slots, number):
        for block in range(4):
            slots[c, :, pl.ds(128 * block, 128)] = jnp.sum(
                q[pl.ds(128 * block, 128), :].T, axis=0, keepdims=True
            )
        return [
            send(slots.at[c], slots.at[c], number + k - 1, (s, c_peer(k))) for k in range(1, NC)
        ]

    def spread(row, columns):
        for block in range(4):
            columns[pl.ds(128 * block, 128), :] = jnp.broadcast_to(
                row[:, 128 * block : 128 * block + 128], (128, 128)
            ).T

    got_sq = row_sums(sqs, S_SQ)
    for a in range(3):
        for b in range(6):
            tile = act[pl.ds(16 + 128 * a, 128), pl.ds(128 * b, 128)].astype(F32)
            actt[pl.ds(128 * b, 128), pl.ds(128 * a, 128)] = tile.T.astype(BF16)
    load_cot.wait()
    arrived(got_cot)
    arrived(got_sq)
    spread(
        lax.rsqrt((sqs[0] + sqs[1] + sqs[2] + sqs[3]) * (1.0 / D2) + EPS), s2
    )
    g2acc[...] = jnp.zeros_like(g2acc)

    def second_norm(rows, cot, own, count):
        scale = s2[rows, :]
        scale = jnp.concatenate([scale, scale], axis=1)
        normed = c2[rows, :] * scale
        gain = g2_ref[...]
        pre = normed * gain
        cdf, slope = gelu_parts(pre)
        dpre = cot * slope
        dnormed = dpre * gain
        inner = dnormed * normed
        c2[rows, :] = normed
        dn2[rows, :] = dnormed
        q[rows, :] = inner[:, :128] + inner[:, 128:]
        if own is not None:
            feat_ref[own, :] = (pre * cdf).astype(BF16)
            g2acc[...] += jnp.sum(dpre * normed, axis=0, keepdims=True)

    second_norm(pl.ds(8, 8), cext[pl.ds(0, 16), :].astype(F32)[8:16], None, 8)
    second_norm(pl.ds(400, 8), cext[pl.ds(400, 16), :].astype(F32)[0:8], None, 8)

    @pl.loop(0, 8)
    def _(i):
        rows = pl.ds(pl.multiple_of(16 + i * 48, 16), 48)
        own = pl.ds(pl.multiple_of(i * 48, 16), 48)
        second_norm(rows, cext[rows, :].astype(F32), own, 48)

    got_in = row_sums(ins, S_IN)
    arrived(got_in)
    spread((ins[0] + ins[1] + ins[2] + ins[3]) * (1.0 / D2), m2)

    for start, count in pieces:
        rows = pl.ds(start, count)
        scale, mean = s2[rows, :], m2[rows, :]
        scale = jnp.concatenate([scale, scale], axis=1)
        mean = jnp.concatenate([mean, mean], axis=1)
        grad = scale * (dn2[rows, :] - c2[rows, :] * mean)
        if start == 8:
            grad = jnp.where(s > 0, grad, 0.0)
        if start == 400:
            grad = jnp.where(s < NS - 1, grad, 0.0)
        d2[rows, :] = grad
    for tap in range(KW2):
        for k in range(8):
            dcat[pl.ds(48 * k, 48), pl.ds(256 * tap, 256)] = d2[
                pl.ds(48 * k + 18 - tap, 48), :
            ].astype(BF16)

    to_core = (s, zh * 2 + 1 - core)
    to_zhi = (s, (1 - zh) * 2 + core)
    got_core = []
    for j in range(4):
        part_of = lax.rem(zh + 1 - j // 2, 2) * 2 + lax.rem(core + 1 - j % 2, 2)
        rows = pl.ds(pl.multiple_of(part_of * PART, 32), PART)
        total = nt_dot(dcat[rows, pl.ds(0, 256)], w2v[0])
        for tap in range(1, KW2):
            total = total + nt_dot(dcat[rows, pl.ds(256 * tap, 256)], w2v[tap])
        pb[j] = total.astype(BF16)
        if j % 2 == 0:
            got_core.append(send(pb.at[j], pcin.at[j // 2], S_CORE + j // 2, to_core))
    arrived(got_core[:1])
    zs_[...] = (pb[1].astype(F32) + pcin[0].astype(F32)).astype(BF16)
    got_zhi = send(zs_, zr_, S_ZHI, to_zhi)

    def ay_copy(k):
        to = lax.rem(y + 1 + k, NY)
        return pltpu.make_async_remote_copy(
            src_ref=big.at[to, :, pl.ds(0, RA), :],
            dst_ref=rya.at[y],
            send_sem=ssem.at[S_AY + k],
            recv_sem=rsem.at[S_AY + k],
            device_id=(seq_of(to, x, z), c),
            device_id_type=MESH,
        )

    @pl.loop(0, NY)
    def _(k):
        to = lax.rem(y + 1 + k, NY)
        part = jnp.dot(
            actt[pl.ds(pl.multiple_of(to * 96, 32), 96), :],
            dcat[...],
            preferred_element_type=F32,
        )
        for xx in range(NX):
            for tap in range(KW2):
                lo = part[24 * xx : 24 * xx + 24, 256 * tap : 256 * tap + 128]
                hi = part[24 * xx : 24 * xx + 24, 256 * tap + 128 : 256 * tap + 256]
                big[to, xx, pl.ds(48 * tap, 48), :] = jnp.concatenate([lo, hi], axis=0).astype(BF16)

        @pl.when(k < NY - 1)
        def _():
            ay_copy(k).start()

    got_ay = [ay_copy(k) for k in range(NY - 1)]
    pending.extend(got_ay)
    got_bx = [
        send(
            big.at[:, x_peer(k), pl.ds(RA, RB), :],
            rxb.at[x],
            S_BX + k - 1,
            (seq_of(y, x_peer(k), z), c),
        )
        for k in range(1, NX)
    ]

    arrived(got_core[1:])
    arrived([got_zhi])
    g1acc[...] = jnp.zeros_like(g1acc)

    @pl.loop(0, PART // 32)
    def _(i):
        local = pl.ds(pl.multiple_of(i * 32, 32), 32)
        rows = pl.ds(pl.multiple_of(16 + c * PART + i * 32, 16), 32)
        dact = pb[3, local, :].astype(F32) + pcin[1, local, :].astype(F32) + zr_[local, :].astype(F32)
        normed = n1[rows, :]
        gain = gain1[...]
        _, slope = gelu_parts(normed * gain)
        dpre = dact * slope
        g1acc[...] += jnp.sum(dpre * normed, axis=0, keepdims=True)
        dnormed = dpre * gain
        mean = jnp.sum(dnormed * normed, axis=1, keepdims=True) * (1.0 / D1)
        dc1[local, :] = (s1[rows, :][:, :1] * (dnormed - normed * mean)).astype(BF16)

    mine = pl.ds(pl.multiple_of(16 + c * PART, 16), PART)
    pay[...] = tn_dot(uu[mine, :], dc1[...])
    pay[pl.ds(60, 1), :] = g1acc[...]
    for k in range(NC):
        chs[k, :, pl.ds(0, 128)] = pay[:, OWN1 * k : OWN1 * k + 128].astype(BF16)
        chs[k, :, pl.ds(128, 128)] = jnp.concatenate(
            [pay[:, OWN1 * k + 128 : OWN1 * k + 192], jnp.zeros((64, 64), F32)], axis=1
        ).astype(BF16)
    got_ch = [
        send(chs.at[c_peer(k)], chr_.at[c], S_CH + k - 1, (s, c_peer(k))) for k in range(1, NC)
    ]
    chr_[c] = chs[c]

    def add_up(slots, count):
        total = slots[0].astype(F32)
        for k in range(1, count):
            total = total + slots[k].astype(F32)
        return total

    rya[y] = big[y, :, pl.ds(0, RA), :]
    arrived(got_ay)

    @pl.loop(0, NX)
    def _(i):
        total = rya[0, i].astype(F32)
        for k in range(1, NY):
            total = total + rya[k, i].astype(F32)
        a2[i] = total.astype(BF16)

    got_ax = [
        send(a2.at[x_peer(k)], rxa.at[x], S_AX + k - 1, (seq_of(y, x_peer(k), z), c))
        for k in range(1, NX)
    ]
    rxa[x] = a2[x]
    rxb[x] = big[:, x, pl.ds(RA, RB), :]
    arrived(got_bx)

    @pl.loop(0, NY)
    def _(i):
        total = rxb[0, i].astype(F32)
        for k in range(1, NX):
            total = total + rxb[k, i].astype(F32)
        b2[i] = total.astype(BF16)

    got_by = [
        send(b2.at[y_peer(k)], ryb.at[y], S_BY + k - 1, (seq_of(y_peer(k), x, z), c))
        for k in range(1, NY)
    ]
    ryb[y] = b2[y]

    arrived(got_ch)
    small = add_up(chr_, NC)
    pay[:, pl.ds(0, 256)] = small
    pay[pl.ds(61, 1), pl.ds(0, 128)] = g2acc[:, :128]
    pay[pl.ds(62, 1), pl.ds(0, 128)] = g2acc[:, 128:]
    axs[x] = pay[:, pl.ds(0, 256)].astype(BF16)
    got_rx = [
        send(axs.at[x], axs.at[x], S_RX + k - 1, (seq_of(y, x_peer(k), z), c)) for k in range(1, NX)
    ]
    arrived(got_ax)
    fin[pl.ds(0, RA), :] = add_up(rxa, NX)
    arrived(got_rx)
    ays[y] = add_up(axs, NX).astype(BF16)
    got_ry = [
        send(ays.at[y], ays.at[y], S_RY + k - 1, (seq_of(y_peer(k), x, z), c)) for k in range(1, NY)
    ]
    arrived(got_by)
    fin[pl.ds(RA, RB), :] = add_up(ryb, NY)
    fin[pl.ds(CHUNK, 8), :] = jnp.zeros((8, 128), F32)
    for zz in range(NZ):
        for u in range(KW2):
            zsl[zz, pl.ds(16 * u, 16), :] = jnp.concatenate(
                [fin[pl.ds(48 * u + 6 * zz, 8), :], fin[pl.ds(48 * u + 24 + 6 * zz, 8), :]], axis=0
            ).astype(BF16)
    got_z = [
        send(zsl.at[z_peer(k)], rzl.at[z], S_Z + k - 1, (seq_of(y, x, z_peer(k)), c))
        for k in range(1, NZ)
    ]
    rzl[z] = zsl[z]
    arrived(got_ry)
    azs[z] = add_up(ays, NY).astype(BF16)
    got_rz = [
        send(azs.at[z], azs.at[z], S_RZ + k - 1, (seq_of(y, x, z_peer(k)), c)) for k in range(1, NZ)
    ]
    arrived(got_z)
    total = add_up(rzl, NZ)
    for tap in range(KW2):
        for half in range(2):
            gw2_ref[tap, :, pl.ds(128 * half, 128)] = total[16 * tap + 8 * half : 16 * tap + 8 * half + 6]
    arrived(got_rz)
    total = add_up(azs, NZ)
    gw1_ref[...] = total[:60, :OWN1]
    gg1_ref[...] = total[60:61, :OWN1]
    gg2_ref[:, pl.ds(0, 128)] = total[61:62, :128]
    gg2_ref[:, pl.ds(128, 128)] = total[62:63, :128]
    for copy in pending:
        copy.wait_send()


def on_device(bases, conv1_weight, gain1, conv2_weight, gain2, cotangent):
    w1 = conv1_weight.transpose(1, 0, 2).reshape(KW1 * BASES, OWN1)
    w1 = jnp.pad(w1, ((0, 4), (0, 64)))
    g1 = jnp.pad(gain1.reshape(1, OWN1), ((0, 0), (0, 64)))
    vmem = pl.BlockSpec(memory_space=pltpu.VMEM)
    hbm = pl.BlockSpec(memory_space=pl.ANY)
    V = pltpu.VMEM
    outs = pl.pallas_call(
        kernel,
        out_shape=(
            jax.ShapeDtypeStruct((ROWS, OWN2), BF16),
            jax.ShapeDtypeStruct((KW1 * BASES, OWN1), F32),
            jax.ShapeDtypeStruct((1, OWN1), F32),
            jax.ShapeDtypeStruct((KW2, 6, OWN2), F32),
            jax.ShapeDtypeStruct((1, OWN2), F32),
        ),
        in_specs=[vmem, vmem, vmem, hbm, vmem, hbm],
        out_specs=(vmem,) * 5,
        scratch_shapes=[
            V((1, 640), jnp.int32),
            V((FRAME, OWN2), BF16),
            V((NC, 64, 256), BF16),
            V((NC, 1, 256), F32),
            V((1, D1), F32),
            V((64, D1), BF16),
            V((64, 512), F32),
            V((512, 64), BF16),
            V((FRAME, D1), F32),
            V((FRAME, 128), F32),
            V((FRAME, D1), BF16),
            V((D1, ROWS), BF16),
            V((KW2, D1, OWN2), BF16),
            V((KW2, FRAME, OWN2), F32),
            V((FRAME, OWN2), F32),
            V((FRAME, OWN2), F32),
            V((512, 128), F32),
            V((512, 128), F32),
            V((512, 128), F32),
            V((NC, 1, 512), F32),
            V((NC, 1, 512), F32),
            V((FRAME, OWN2), F32),
            V((ROWS, KW2 * OWN2), BF16),
            V((1, OWN2), F32),
            V((1, D1), F32),
            V((4, PART, D1), BF16),
            V((2, PART, D1), BF16),
            V((PART, D1), BF16),
            V((PART, D1), BF16),
            V((PART, D1), BF16),
            V((64, D1), F32),
            V((NC, 64, 256), BF16),
            V((NC, 64, 256), BF16),
            V((NX, 64, 256), BF16),
            V((NY, 64, 256), BF16),
            V((NZ, 64, 256), BF16),
            V((NY, NX, CHUNK, 128), BF16),
            V((NY, NX, RA, 128), BF16),
            V((NX, NY, RB, 128), BF16),
            V((NX, RA, 128), BF16),
            V((NY, RB, 128), BF16),
            V((NX, RA, 128), BF16),
            V((NY, RB, 128), BF16),
            V((CHUNK + 8, 128), F32),
            V((NZ, 80, 128), BF16),
            V((NZ, 80, 128), BF16),
            pltpu.SemaphoreType.DMA((N_SEM,)),
            pltpu.SemaphoreType.DMA((N_SEM,)),
            pltpu.SemaphoreType.DMA((2,)),
        ],
        compiler_params=pltpu.CompilerParams(
            collective_id=0, has_side_effects=True, vmem_limit_bytes=44 * 1024 * 1024
        ),
        cost_estimate=pl.CostEstimate(
            flops=3 * 2 * ROWS * D1 * KW2 * OWN2, bytes_accessed=4 << 20, transcendentals=1 << 20
        ),
    )(
        bases.reshape(1, ROWS),
        w1,
        g1,
        conv2_weight.transpose(1, 0, 2),
        gain2.reshape(1, OWN2),
        cotangent,
    )
    features, gw1, gg1, gw2, gg2 = outs
    grad_w1 = gw1.reshape(KW1, BASES, OWN1).transpose(1, 0, 2)
    return (features, grad_w1, gg1.reshape(OWN1), gw2.transpose(1, 0, 2), gg2.reshape(OWN2))


def solution(mesh):
    in_specs = (
        P("seq"),
        P(None, None, "ch"),
        P("ch"),
        P(None, None, "ch"),
        P("ch"),
        P("seq", "ch"),
    )
    out_specs = (P("seq", "ch"), P(None, None, "ch"), P("ch"), P("seq", None, "ch"), P("ch"))
    return jax.shard_map(
        on_device, mesh=mesh, in_specs=in_specs, out_specs=out_specs, check_vma=False
    )
```

```python
import math

import jax
import jax.numpy as jnp
from jax import lax
from jax.experimental import pallas as pl
from jax.experimental.pallas import tpu as pltpu
from jax.sharding import PartitionSpec as P

BASES = 4
KW1 = 15
KW2 = 5
D1 = 768
D2 = 1024
OWN1 = 192
OWN2 = 256
ROWS = 384
FRAME = 416
NX, NY, NZ, NC = 4, 8, 4, 4
NS = NX * NY * NZ
TAPS1 = KW1 * BASES
WIDE = KW2 * OWN2
HALF = WIDE // 2
SHARE = D1 // NX
EPS = 1e-06
MESH = pl.DeviceIdType.MESH
F32 = jnp.float32
BF16 = jnp.bfloat16
ROOT = math.sqrt(2.0 / math.pi)

S_BASE, S_COT, S_W1, S_G1 = 0, 2, 4, 7
S_SQ, S_IN, S_CH = 10, 13, 16
S_ACT, S_D2, S_GY, S_Z = 19, 22, 28, 42
S_RX, S_RY, S_RZ, S_RG = 45, 48, 55, 58
N_SEM = 61


def gelu_parts(v):
    square = v * v
    t = jnp.tanh(ROOT * (v + 0.044715 * (square * v)))
    cdf = 0.5 * (1.0 + t)
    slope = cdf + (0.5 * ROOT) * v * (1.0 - t * t) * (1.0 + (3.0 * 0.044715) * square)
    return cdf, slope


def nt_dot(a, b):
    return lax.dot_general(a, b, (((1,), (1,)), ((), ())), preferred_element_type=F32)


def tn_dot(a, b):
    return lax.dot_general(a, b, (((0,), (0,)), ((), ())), preferred_element_type=F32)


def kernel(
    bases_hbm, w1_hbm, g1_hbm, w2_ref, g2_hbm, cot_ref,
    feat_ref, gw1_ref, gg1_ref, gw2_ref, gg2_ref,
    bases_ref, g1_ref, g2_ref, bext, cext, w1g, g1g, gain1, gain2, w1full, ut, uu, n1, s1, h1, act, actt, asel, aget,
    w2v, ybuf, c2, dn2, q, s2, m2, sqs, ins, d2, d2s, d2f, dcat, g2acc, g1acc,
    dact, dc1, pay, chs, chr_, rsend, rxs, rys, rzs, rgs,
    part, big, ryg, fin, zsl, rzl,
    ssem, rsem, lsem,
):
    s = lax.axis_index("seq")
    c = lax.axis_index("ch")
    z = lax.rem(s, NZ)
    x = lax.rem(lax.div(s, NZ), NX)
    y = lax.div(s, NZ * NX)

    def seq_of(yy, xx, zz):
        return (yy * NX + xx) * NZ + zz

    def x_peer(k):
        return lax.rem(x + k, NX)

    def y_peer(k):
        return lax.rem(y + k, NY)

    def z_peer(k):
        return lax.rem(z + k, NZ)

    def c_peer(k):
        return lax.rem(c + k, NC)

    right = lax.rem(s + 1, NS)
    left = lax.rem(s + NS - 1, NS)

    first_loads = [
        pltpu.make_async_copy(bases_hbm, bases_ref, lsem.at[11]),
        pltpu.make_async_copy(w1_hbm, w1g.at[c], lsem.at[12]),
        pltpu.make_async_copy(g1_hbm, g1_ref, lsem.at[13]),
        pltpu.make_async_copy(g2_hbm, g2_ref, lsem.at[14]),
    ]
    for load in first_loads:
        load.start()
    loads = []
    for half in range(2):
        for tap in range(KW2):
            n = half * KW2 + tap
            loads.append(
                pltpu.make_async_copy(
                    w2_ref.at[tap, :, pl.ds(128 * half, 128)],
                    w2v.at[:, pl.ds(128 * n, 128)],
                    lsem.at[n],
                )
            )
    for load in loads:
        load.start()
    load_cot = pltpu.make_async_copy(cot_ref, cext.at[pl.ds(16, ROWS)], lsem.at[10])
    load_cot.start()

    barrier = pltpu.get_barrier_semaphore()
    friends = [(right, c), (left, c)]
    friends += [(s, c_peer(k)) for k in range(1, NC)]
    friends += [(seq_of(y, x_peer(k), z), c) for k in range(1, NX)]
    friends += [(seq_of(y_peer(k), x, z), c) for k in range(1, NY)]
    friends += [(seq_of(y, x, z_peer(k)), c) for k in range(1, NZ)]
    for friend in friends:
        pl.semaphore_signal(barrier, inc=1, device_id=friend, device_id_type=MESH)
    for load in first_loads:
        load.wait()
    bext[:, pl.ds(128, ROWS)] = bases_ref[...].reshape(1, ROWS)
    g1g[c] = g1_ref[...].reshape(1, OWN1)
    gain2[...] = g2_ref[...].reshape(1, OWN2)
    pl.semaphore_wait(barrier, len(friends))

    pending = []

    def send(src, dst, number, to):
        copy = pltpu.make_async_remote_copy(
            src_ref=src,
            dst_ref=dst,
            send_sem=ssem.at[number],
            recv_sem=rsem.at[number],
            device_id=to,
            device_id_type=MESH,
        )
        copy.start()
        pending.append(copy)
        return copy

    def arrived(copies):
        for copy in copies:
            copy.wait_recv()

    got_bases = [
        send(bext.at[:, pl.ds(384, 128)], bext.at[:, pl.ds(0, 128)], S_BASE, (right, c)),
        send(bext.at[:, pl.ds(128, 128)], bext.at[:, pl.ds(512, 128)], S_BASE + 1, (left, c)),
    ]
    got_w1 = []
    for k in (2, 1, 3):
        to = (s, c_peer(k))
        got_w1.append(send(w1g.at[c], w1g.at[c], S_W1 + k - 1, to))
        got_w1.append(send(g1g.at[c], g1g.at[c], S_G1 + k - 1, to))
    got_cot = [
        send(cot_ref.at[pl.ds(ROWS - 16, 16)], cext.at[pl.ds(0, 16)], S_COT, (right, c)),
        send(cot_ref.at[pl.ds(0, 16)], cext.at[pl.ds(16 + ROWS, 16)], S_COT + 1, (left, c)),
    ]

    arrived(got_bases)
    place = lax.broadcasted_iota(jnp.int32, (1, 640), 1) - 128 + s * ROWS
    known = jnp.where((place >= 0) & (place < NS * ROWS), bext[...], -1)
    kinds = lax.broadcasted_iota(jnp.int32, (BASES, 512), 0)
    for tap in range(KW1):
        rolled = pltpu.roll(known, 640 - (105 + tap), 1)[:, :512]
        ut[pl.ds(BASES * tap, BASES), :] = (
            jnp.broadcast_to(rolled, (BASES, 512)) == kinds
        ).astype(F32)
    ut[pl.ds(BASES * KW1, 4), :] = jnp.zeros((4, 512), F32)
    for block in range(4):
        uu[pl.ds(128 * block, 128), :] = ut[:, pl.ds(128 * block, 128)].T.astype(BF16)

    arrived(got_w1)
    w1full[pl.ds(0, TAPS1), :] = jnp.concatenate(
        [w1g[k].astype(F32).reshape(TAPS1, OWN1) for k in range(NC)], axis=1
    ).astype(BF16)
    w1full[pl.ds(TAPS1, 4), :] = jnp.zeros((4, D1), BF16)
    gain1[...] = jnp.concatenate([g1g[k] for k in range(NC)], axis=1)
    n1[...] = jnp.dot(uu[pl.ds(0, FRAME), :], w1full[...], preferred_element_type=F32)

    @pl.loop(0, FRAME // 32)
    def _(i):
        rows = pl.ds(pl.multiple_of(i * 32, 32), 32)
        v = n1[rows, :]
        scale = lax.rsqrt(jnp.sum(v * v, axis=1, keepdims=True) * (1.0 / D1) + EPS)
        normed = v * scale
        n1[rows, :] = normed
        s1[rows, :] = jnp.broadcast_to(scale, (32, 128))
        pre = normed * gain1[...]
        cdf, _ = gelu_parts(pre)
        where = lax.broadcasted_iota(jnp.int32, (32, 1), 0) + (i * 32 - 16) + s * ROWS
        inside = (where >= 0) & (where < NS * ROWS)
        act[rows, :] = jnp.where(inside, pre * cdf, 0.0).astype(BF16)

    for load in loads:
        load.wait()
    ybuf[...] = jnp.dot(act[...], w2v[...], preferred_element_type=F32)
    pieces = [(8, 8)] + [(16 + 48 * k, 48) for k in range(8)] + [(400, 8)]
    q[pl.ds(0, 8), :] = jnp.zeros((8, 128), F32)
    q[pl.ds(408, 104), :] = jnp.zeros((104, 128), F32)
    for start, count in pieces:
        squares = None
        for half in range(2):
            total = None
            for tap in range(KW2):
                term = ybuf[
                    pl.ds(start + tap - 2, count), pl.ds(128 * (half * KW2 + tap), 128)
                ]
                total = term if total is None else total + term
            c2[pl.ds(start, count), pl.ds(128 * half, 128)] = total
            squares = total * total if squares is None else squares + total * total
        q[pl.ds(start, count), :] = squares
    def row_sums(slots, number):
        for block in range(4):
            slots[c, :, pl.ds(128 * block, 128)] = jnp.sum(
                q[pl.ds(128 * block, 128), :].T, axis=0, keepdims=True
            )
        return [
            send(slots.at[c], slots.at[c], number + k - 1, (s, c_peer(k))) for k in (2, 1, 3)
        ]

    def spread(row, columns):
        for block in range(4):
            columns[pl.ds(128 * block, 128), :] = jnp.broadcast_to(
                row[:, 128 * block : 128 * block + 128], (128, 128)
            ).T

    got_sq = row_sums(sqs, S_SQ)
    for a in range(3):
        for b in range(6):
            tile = act[pl.ds(16 + 128 * a, 128), pl.ds(128 * b, 128)].astype(F32)
            actt[pl.ds(128 * b, 128), pl.ds(128 * a, 128)] = tile.T
    for xx in range(NX):
        for yy in range(0, NY, 2):
            asel[xx, pl.ds(24 * yy, 48), :] = jnp.concatenate(
                [
                    actt[pl.ds(96 * yy + 24 * xx, 24), :],
                    actt[pl.ds(96 * yy + 96 + 24 * xx, 24), :],
                ],
                axis=0,
            ).astype(BF16)
    got_act = [
        send(asel.at[x_peer(k)], aget.at[x], S_ACT + k - 1, (seq_of(y, x_peer(k), z), c))
        for k in range(1, NX)
    ]
    aget[x] = asel[x]

    @pl.loop(0, ROWS // 32)
    def _(i):
        local = pl.ds(pl.multiple_of(i * 32, 32), 32)
        gain = gain1[...]
        _, slope = gelu_parts(n1[pl.ds(pl.multiple_of(i * 32 + 16, 16), 32), :] * gain)
        h1[local, :] = slope * gain

    load_cot.wait()
    arrived(got_cot)
    arrived(got_sq)
    spread(
        lax.rsqrt((sqs[0] + sqs[1] + sqs[2] + sqs[3]) * (1.0 / D2) + EPS), s2
    )
    g2acc[...] = jnp.zeros_like(g2acc)

    def second_norm(rows, cot, own, count):
        scale = s2[rows, :]
        scale = jnp.concatenate([scale, scale], axis=1)
        normed = c2[rows, :] * scale
        gain = gain2[...]
        pre = normed * gain
        cdf, slope = gelu_parts(pre)
        dpre = cot * slope
        dnormed = dpre * gain
        inner = dnormed * normed
        c2[rows, :] = normed
        dn2[rows, :] = dnormed
        q[rows, :] = inner[:, :128] + inner[:, 128:]
        if own is not None:
            feat_ref[own, :] = (pre * cdf).astype(BF16)
            g2acc[...] += jnp.sum(dpre * normed, axis=0, keepdims=True)

    second_norm(pl.ds(8, 8), cext[pl.ds(0, 16), :].astype(F32)[8:16], None, 8)
    second_norm(pl.ds(400, 8), cext[pl.ds(400, 16), :].astype(F32)[0:8], None, 8)

    @pl.loop(0, 8)
    def _(i):
        rows = pl.ds(pl.multiple_of(16 + i * 48, 16), 48)
        own = pl.ds(pl.multiple_of(i * 48, 16), 48)
        second_norm(rows, cext[rows, :].astype(F32), own, 48)

    got_in = row_sums(ins, S_IN)
    arrived(got_in)
    spread((ins[0] + ins[1] + ins[2] + ins[3]) * (1.0 / D2), m2)

    def rows_of(b):
        return pl.ds(pl.multiple_of(b * ROWS, 128), ROWS)

    def expand(b, half):
        for tap in range(KW2):
            for k in range(8):
                dcat[
                    pl.ds(pl.multiple_of(b * ROWS + 48 * k, 16), 48),
                    pl.ds(128 * (half * KW2 + tap), 128),
                ] = d2f[pl.ds(48 * k + 18 - tap, 48), :].astype(BF16)

    got_d2 = []
    for half in range(2):
        columns = pl.ds(128 * half, 128)
        d2[half, pl.ds(0, 8), :] = jnp.zeros((8, 128), F32)
        d2[half, pl.ds(408, 8), :] = jnp.zeros((8, 128), F32)
        for start, count in pieces:
            rows = pl.ds(start, count)
            grad = s2[rows, :] * (dn2[rows, columns] - c2[rows, columns] * m2[rows, :])
            if start == 8:
                grad = jnp.where(s > 0, grad, 0.0)
            if start == 400:
                grad = jnp.where(s < NS - 1, grad, 0.0)
            d2[half, rows, :] = grad
        d2s[x, half] = d2[half].astype(BF16)
        got_d2.append(
            [
                send(
                    d2s.at[x, half],
                    d2s.at[x, half],
                    S_D2 + 3 * half + k - 1,
                    (seq_of(y, x_peer(k), z), c),
                )
                for k in range(1, NX)
            ]
        )
    for half in range(2):
        d2f[...] = d2[half]
        expand(x, half)
    dact[...] = nt_dot(dcat[rows_of(x), :], w2v[...]).astype(BF16)
    g1acc[...] = jnp.zeros_like(g1acc)

    @pl.loop(0, ROWS // 32)
    def _(i):
        local = pl.ds(pl.multiple_of(i * 32, 32), 32)
        rows = pl.ds(pl.multiple_of(16 + i * 32, 16), 32)
        normed = n1[rows, :]
        dnormed = dact[local, :].astype(F32) * h1[local, :]
        inner = dnormed * normed
        g1acc[...] += jnp.sum(inner, axis=0, keepdims=True)
        mean = jnp.sum(inner, axis=1, keepdims=True) * (1.0 / D1)
        dc1[local, :] = (s1[rows, :][:, :1] * (dnormed - normed * mean)).astype(BF16)

    pay[...] = tn_dot(uu[pl.ds(16, ROWS), :], dc1[...])
    pay[pl.ds(60, 1), :] = g1acc[...] / gain1[...]
    for k in range(NC):
        chs[k, :, pl.ds(0, 128)] = pay[:, OWN1 * k : OWN1 * k + 128].astype(BF16)
        chs[k, :, pl.ds(128, 128)] = jnp.concatenate(
            [pay[:, OWN1 * k + 128 : OWN1 * k + 192], jnp.zeros((64, 64), F32)], axis=1
        ).astype(BF16)
    got_ch = [
        send(chs.at[c_peer(k)], chr_.at[c], S_CH + k - 1, (s, c_peer(k))) for k in (2, 1, 3)
    ]
    chr_[c] = chs[c]

    def add_up(slots, count):
        total = slots[0].astype(F32)
        for k in range(1, count):
            total = total + slots[k].astype(F32)
        return total

    def half_grad(half):
        arrived(got_d2[half])
        for k in range(1, NX):
            b = x_peer(k)
            d2f[...] = d2s[b, half].astype(F32)
            expand(b, half)
        columns = pl.ds(HALF * half, HALF)
        total = jnp.dot(aget[0], dcat[pl.ds(0, ROWS), columns], preferred_element_type=F32)
        for b in range(1, NX):
            total = total + jnp.dot(
                aget[b], dcat[pl.ds(ROWS * b, ROWS), columns], preferred_element_type=F32
            )
        part[...] = total
        for yy in range(NY):
            rows = pl.ds(24 * yy, 24)
            taps = [part[rows, pl.ds(128 * tap, 128)] for tap in range(KW2)]
            taps.append(jnp.zeros((8, 128), F32))
            for first in (0, 2, 4):
                piece = jnp.concatenate(taps[first : first + 2], axis=0).astype(BF16)
                big[half, yy, pl.ds(24 * first, piece.shape[0]), :] = piece
        copies = [
            send(
                big.at[half, y_peer(k)],
                ryg.at[half, y],
                S_GY + 7 * half + k - 1,
                (seq_of(y_peer(k), x, z), c),
            )
            for k in (4, 3, 5, 2, 6, 1, 7)
        ]
        ryg[half, y] = big[half, y]
        return copies

    arrived(got_act)
    got_y0 = half_grad(0)
    arrived(got_ch)
    pay[:, pl.ds(0, 256)] = add_up(chr_, NC)
    pay[pl.ds(61, 1), pl.ds(0, 128)] = g2acc[:, :128]
    pay[pl.ds(62, 1), pl.ds(0, 128)] = g2acc[:, 128:]
    for k in range(NX):
        rsend[k] = pay[pl.ds(16 * k, 16), pl.ds(0, 256)].astype(BF16)
    got_rx = [
        send(rsend.at[x_peer(k)], rxs.at[x], S_RX + k - 1, (seq_of(y, x_peer(k), z), c))
        for k in range(1, NX)
    ]
    rxs[x] = rsend[x]
    got_y1 = half_grad(1)
    arrived(got_rx)
    rys[y] = add_up(rxs, NX).astype(BF16)
    got_ry = [
        send(rys.at[y], rys.at[y], S_RY + k - 1, (seq_of(y_peer(k), x, z), c)) for k in range(1, NY)
    ]

    def half_sum(half):
        total = ryg[half, 0].astype(F32)
        for k in range(1, NY):
            total = total + ryg[half, k].astype(F32)
        fin[half] = total

    arrived(got_y0)
    half_sum(0)
    arrived(got_ry)
    rzs[z] = add_up(rys, NY).astype(BF16)
    got_rz = [
        send(rzs.at[z], rzs.at[z], S_RZ + k - 1, (seq_of(y, x, z_peer(k)), c)) for k in range(1, NZ)
    ]
    arrived(got_y1)
    half_sum(1)
    for zz in range(NZ):
        for tap in range(KW2):
            rows = pl.ds(24 * tap + 6 * zz, 8)
            zsl[zz, pl.ds(16 * tap, 16), :] = jnp.concatenate(
                [fin[0, rows, :], fin[1, rows, :]], axis=0
            ).astype(BF16)
    got_z = [
        send(zsl.at[z_peer(k)], rzl.at[z], S_Z + k - 1, (seq_of(y, x, z_peer(k)), c))
        for k in range(1, NZ)
    ]
    rzl[z] = zsl[z]
    arrived(got_rz)
    rgs[x] = add_up(rzs, NZ)
    got_rg = [
        send(rgs.at[x], rgs.at[x], S_RG + k - 1, (seq_of(y, x_peer(k), z), c)) for k in range(1, NX)
    ]
    arrived(got_z)
    total = add_up(rzl, NZ)
    for tap in range(KW2):
        for half in range(2):
            gw2_ref[tap, :, pl.ds(128 * half, 128)] = total[16 * tap + 8 * half : 16 * tap + 8 * half + 6]
    arrived(got_rg)
    for k in range(NX):
        for j in range(4):
            tap = 4 * k + j
            if tap < KW1:
                gw1_ref[tap] = rgs[k, pl.ds(4 * j, 4), pl.ds(0, OWN1)]
    gg1_ref[...] = rgs[3, pl.ds(12, 1), pl.ds(0, OWN1)].reshape(OWN1)
    gg2_ref[...] = jnp.concatenate(
        [rgs[3, pl.ds(13, 1), pl.ds(0, 128)], rgs[3, pl.ds(14, 1), pl.ds(0, 128)]], axis=1
    ).reshape(OWN2)
    for copy in pending:
        copy.wait_send()


def on_device(bases, conv1_weight, gain1, conv2_weight, gain2, cotangent):
    vmem = pl.BlockSpec(memory_space=pltpu.VMEM)
    hbm = pl.BlockSpec(memory_space=pl.ANY)
    V = pltpu.VMEM
    features, gw1, gg1, gw2, gg2 = pl.pallas_call(
        kernel,
        out_shape=(
            jax.ShapeDtypeStruct((ROWS, OWN2), BF16),
            jax.ShapeDtypeStruct((KW1, BASES, OWN1), F32),
            jax.ShapeDtypeStruct((OWN1,), F32),
            jax.ShapeDtypeStruct((KW2, 6, OWN2), F32),
            jax.ShapeDtypeStruct((OWN2,), F32),
        ),
        in_specs=[hbm] * 6,
        out_specs=(vmem,) * 5,
        scratch_shapes=[
            V((ROWS,), jnp.int32),
            V((OWN1,), F32),
            V((OWN2,), F32),
            V((1, 640), jnp.int32),
            V((FRAME, OWN2), BF16),
            V((NC, KW1, BASES, OWN1), BF16),
            V((NC, 1, OWN1), F32),
            V((1, D1), F32),
            V((1, OWN2), F32),
            V((64, D1), BF16),
            V((64, 512), F32),
            V((512, 64), BF16),
            V((FRAME, D1), F32),
            V((FRAME, 128), F32),
            V((ROWS, D1), F32),
            V((FRAME, D1), BF16),
            V((D1, ROWS), F32),
            V((NX, SHARE, ROWS), BF16),
            V((NX, SHARE, ROWS), BF16),
            V((D1, WIDE), BF16),
            V((FRAME, WIDE), F32),
            V((FRAME, OWN2), F32),
            V((FRAME, OWN2), F32),
            V((512, 128), F32),
            V((512, 128), F32),
            V((512, 128), F32),
            V((NC, 1, 512), F32),
            V((NC, 1, 512), F32),
            V((2, FRAME, 128), F32),
            V((NX, 2, FRAME, 128), BF16),
            V((FRAME, 128), F32),
            V((NX * ROWS, WIDE), BF16),
            V((1, OWN2), F32),
            V((1, D1), F32),
            V((ROWS, D1), BF16),
            V((ROWS, D1), BF16),
            V((64, D1), F32),
            V((NC, 64, 256), BF16),
            V((NC, 64, 256), BF16),
            V((NX, 16, 256), BF16),
            V((NX, 16, 256), BF16),
            V((NY, 16, 256), BF16),
            V((NZ, 16, 256), BF16),
            V((NX, 16, 256), F32),
            V((SHARE, HALF), F32),
            V((2, NY, 128, 128), BF16),
            V((2, NY, 128, 128), BF16),
            V((2, 128, 128), F32),
            V((NZ, 80, 128), BF16),
            V((NZ, 80, 128), BF16),
            pltpu.SemaphoreType.DMA((N_SEM,)),
            pltpu.SemaphoreType.DMA((N_SEM,)),
            pltpu.SemaphoreType.DMA((15,)),
        ],
        compiler_params=pltpu.CompilerParams(
            collective_id=0, has_side_effects=True, vmem_limit_bytes=58 * 1024 * 1024
        ),
        cost_estimate=pl.CostEstimate(
            flops=3 * 2 * ROWS * D1 * KW2 * OWN2, bytes_accessed=4 << 20, transcendentals=1 << 20
        ),
    )(
        bases,
        conv1_weight.transpose(1, 0, 2),
        gain1,
        conv2_weight.transpose(1, 0, 2),
        gain2,
        cotangent,
    )
    return (features, gw1.transpose(1, 0, 2), gg1, gw2.transpose(1, 0, 2), gg2)


def solution(mesh):
    in_specs = (
        P("seq"),
        P(None, None, "ch"),
        P("ch"),
        P(None, None, "ch"),
        P("ch"),
        P("seq", "ch"),
    )
    out_specs = (P("seq", "ch"), P(None, None, "ch"), P("ch"), P("seq", None, "ch"), P("ch"))
    return jax.shard_map(
        on_device, mesh=mesh, in_specs=in_specs, out_specs=out_specs, check_vma=False
    )
```

```python
import math

import jax
import jax.numpy as jnp
from jax import lax
from jax.experimental import pallas as pl
from jax.experimental.pallas import tpu as pltpu
from jax.sharding import PartitionSpec as P

BASES = 4
KW1 = 15
KW2 = 5
D1 = 768
D2 = 1024
OWN1 = 192
OWN2 = 256
ROWS = 384
FRAME = 416
NX, NY, NZ, NC = 4, 8, 4, 4
NS = NX * NY * NZ
TAPS1 = KW1 * BASES
WIDE = KW2 * OWN2
HALF = WIDE // 2
SHARE = D1 // NX
EPS = 1e-06
MESH = pl.DeviceIdType.MESH
F32 = jnp.float32
BF16 = jnp.bfloat16
ROOT = math.sqrt(2.0 / math.pi)

S_BASE, S_COT, S_W1, S_G1 = 0, 2, 4, 7
S_SQ, S_IN, S_CH = 10, 13, 16
S_ACT, S_D2, S_GY, S_Z = 19, 22, 28, 42
S_RX, S_RY, S_RZ, S_RG = 45, 48, 55, 58
N_SEM = 61


def gelu_parts(v):
    square = v * v
    t = jnp.tanh(ROOT * (v + 0.044715 * (square * v)))
    cdf = 0.5 * (1.0 + t)
    slope = cdf + (0.5 * ROOT) * v * (1.0 - t * t) * (1.0 + (3.0 * 0.044715) * square)
    return cdf, slope


def nt_dot(a, b):
    return lax.dot_general(a, b, (((1,), (1,)), ((), ())), preferred_element_type=F32)


def tn_dot(a, b):
    return lax.dot_general(a, b, (((0,), (0,)), ((), ())), preferred_element_type=F32)


def kernel(
    bases_hbm, w1_hbm, g1_hbm, w2_ref, g2_hbm, cot_ref,
    feat_ref, gw1_ref, gg1_ref, gw2_ref, gg2_ref,
    bases_ref, g1_ref, g2_ref, bext, cext, w1g, g1g, gain1, gain2, w1full, ut, uu, n1, s1, h1, act, actt, asel, aget,
    w2v, ybuf, c2, dn2, q, s2, m2, sqs, ins, d2, d2s, d2f, dcat, g2acc, g1acc,
    dact, dc1, pay, chs, chr_, rsend, rxs, rys, rzs, rgs,
    part, big, ryg, fin, zsl, rzl,
    ssem, rsem, lsem,
):
    s = lax.axis_index("seq")
    c = lax.axis_index("ch")
    z = lax.rem(s, NZ)
    x = lax.rem(lax.div(s, NZ), NX)
    y = lax.div(s, NZ * NX)

    def seq_of(yy, xx, zz):
        return (yy * NX + xx) * NZ + zz

    def x_peer(k):
        return lax.rem(x + k, NX)

    def y_peer(k):
        return lax.rem(y + k, NY)

    def z_peer(k):
        return lax.rem(z + k, NZ)

    def c_peer(k):
        return lax.rem(c + k, NC)

    right = lax.rem(s + 1, NS)
    left = lax.rem(s + NS - 1, NS)

    first_loads = [
        pltpu.make_async_copy(bases_hbm, bases_ref, lsem.at[11]),
        pltpu.make_async_copy(w1_hbm, w1g.at[c], lsem.at[12]),
        pltpu.make_async_copy(g1_hbm, g1_ref, lsem.at[13]),
        pltpu.make_async_copy(g2_hbm, g2_ref, lsem.at[14]),
    ]
    for load in first_loads:
        load.start()
    loads = []
    for half in range(2):
        for tap in range(KW2):
            n = half * KW2 + tap
            loads.append(
                pltpu.make_async_copy(
                    w2_ref.at[tap, :, pl.ds(128 * half, 128)],
                    w2v.at[:, pl.ds(128 * n, 128)],
                    lsem.at[n],
                )
            )
    for load in loads:
        load.start()
    load_cot = pltpu.make_async_copy(cot_ref, cext.at[pl.ds(16, ROWS)], lsem.at[10])
    load_cot.start()

    barrier = pltpu.get_barrier_semaphore()
    friends = [(right, c), (left, c)]
    friends += [(s, c_peer(k)) for k in range(1, NC)]
    friends += [(seq_of(y, x_peer(k), z), c) for k in range(1, NX)]
    friends += [(seq_of(y_peer(k), x, z), c) for k in range(1, NY)]
    friends += [(seq_of(y, x, z_peer(k)), c) for k in range(1, NZ)]
    for friend in friends:
        pl.semaphore_signal(barrier, inc=1, device_id=friend, device_id_type=MESH)
    for load in first_loads:
        load.wait()
    bext[:, pl.ds(128, ROWS)] = bases_ref[...].reshape(1, ROWS)
    g1g[c] = g1_ref[...].reshape(1, OWN1)
    gain2[...] = g2_ref[...].reshape(1, OWN2)
    pl.semaphore_wait(barrier, len(friends))

    pending = []

    def send(src, dst, number, to):
        copy = pltpu.make_async_remote_copy(
            src_ref=src,
            dst_ref=dst,
            send_sem=ssem.at[number],
            recv_sem=rsem.at[number],
            device_id=to,
            device_id_type=MESH,
        )
        copy.start()
        pending.append(copy)
        return copy

    def arrived(copies):
        for copy in copies:
            copy.wait_recv()

    got_bases = [
        send(bext.at[:, pl.ds(384, 128)], bext.at[:, pl.ds(0, 128)], S_BASE, (right, c)),
        send(bext.at[:, pl.ds(128, 128)], bext.at[:, pl.ds(512, 128)], S_BASE + 1, (left, c)),
    ]
    got_w1 = []
    for k in (2, 1, 3):
        to = (s, c_peer(k))
        got_w1.append(send(w1g.at[c], w1g.at[c], S_W1 + k - 1, to))
        got_w1.append(send(g1g.at[c], g1g.at[c], S_G1 + k - 1, to))
    got_cot = [
        send(cot_ref.at[pl.ds(ROWS - 16, 16)], cext.at[pl.ds(0, 16)], S_COT, (right, c)),
        send(cot_ref.at[pl.ds(0, 16)], cext.at[pl.ds(16 + ROWS, 16)], S_COT + 1, (left, c)),
    ]

    arrived(got_bases)
    place = lax.broadcasted_iota(jnp.int32, (1, 640), 1) - 128 + s * ROWS
    known = jnp.where((place >= 0) & (place < NS * ROWS), bext[...], -1)
    kinds = lax.broadcasted_iota(jnp.int32, (BASES, 512), 0)
    for tap in range(KW1):
        rolled = pltpu.roll(known, 640 - (105 + tap), 1)[:, :512]
        ut[pl.ds(BASES * tap, BASES), :] = (
            jnp.broadcast_to(rolled, (BASES, 512)) == kinds
        ).astype(F32)
    ut[pl.ds(BASES * KW1, 4), :] = jnp.zeros((4, 512), F32)
    for block in range(4):
        uu[pl.ds(128 * block, 128), :] = ut[:, pl.ds(128 * block, 128)].T.astype(BF16)

    arrived(got_w1)
    w1full[pl.ds(0, TAPS1), :] = jnp.concatenate(
        [w1g[k].astype(F32).reshape(TAPS1, OWN1) for k in range(NC)], axis=1
    ).astype(BF16)
    w1full[pl.ds(TAPS1, 4), :] = jnp.zeros((4, D1), BF16)
    gain1[...] = jnp.concatenate([g1g[k] for k in range(NC)], axis=1)
    n1[...] = jnp.dot(uu[pl.ds(0, FRAME), :], w1full[...], preferred_element_type=F32)

    @pl.loop(0, FRAME // 32)
    def _(i):
        rows = pl.ds(pl.multiple_of(i * 32, 32), 32)
        v = n1[rows, :]
        scale = lax.rsqrt(jnp.sum(v * v, axis=1, keepdims=True) * (1.0 / D1) + EPS)
        normed = v * scale
        n1[rows, :] = normed
        s1[rows, :] = jnp.broadcast_to(scale, (32, 128))
        pre = normed * gain1[...]
        cdf, _ = gelu_parts(pre)
        where = lax.broadcasted_iota(jnp.int32, (32, 1), 0) + (i * 32 - 16) + s * ROWS
        inside = (where >= 0) & (where < NS * ROWS)
        act[rows, :] = jnp.where(inside, pre * cdf, 0.0).astype(BF16)

    for load in loads:
        load.wait()
    ybuf[...] = jnp.dot(act[...], w2v[...], preferred_element_type=F32)
    pieces = [(8, 8)] + [(16 + 48 * k, 48) for k in range(8)] + [(400, 8)]
    q[pl.ds(0, 8), :] = jnp.zeros((8, 128), F32)
    q[pl.ds(408, 104), :] = jnp.zeros((104, 128), F32)
    for start, count in pieces:
        squares = None
        for half in range(2):
            total = None
            for tap in range(KW2):
                term = ybuf[
                    pl.ds(start + tap - 2, count), pl.ds(128 * (half * KW2 + tap), 128)
                ]
                total = term if total is None else total + term
            c2[pl.ds(start, count), pl.ds(128 * half, 128)] = total
            squares = total * total if squares is None else squares + total * total
        q[pl.ds(start, count), :] = squares
    def row_sums(slots, number):
        for block in range(4):
            slots[c, :, pl.ds(128 * block, 128)] = jnp.sum(
                q[pl.ds(128 * block, 128), :].T, axis=0, keepdims=True
            )
        return [
            send(slots.at[c], slots.at[c], number + k - 1, (s, c_peer(k))) for k in (2, 1, 3)
        ]

    def spread(row, columns):
        for block in range(4):
            columns[pl.ds(128 * block, 128), :] = jnp.broadcast_to(
                row[:, 128 * block : 128 * block + 128], (128, 128)
            ).T

    got_sq = row_sums(sqs, S_SQ)
    for a in range(3):
        for b in range(6):
            tile = act[pl.ds(16 + 128 * a, 128), pl.ds(128 * b, 128)].astype(F32)
            actt[pl.ds(128 * b, 128), pl.ds(128 * a, 128)] = tile.T
    for xx in range(NX):
        for yy in range(0, NY, 2):
            asel[xx, pl.ds(24 * yy, 48), :] = jnp.concatenate(
                [
                    actt[pl.ds(96 * yy + 24 * xx, 24), :],
                    actt[pl.ds(96 * yy + 96 + 24 * xx, 24), :],
                ],
                axis=0,
            ).astype(BF16)
    got_act = [
        send(asel.at[x_peer(k)], aget.at[x], S_ACT + k - 1, (seq_of(y, x_peer(k), z), c))
        for k in range(1, NX)
    ]
    aget[x] = asel[x]

    @pl.loop(0, ROWS // 32)
    def _(i):
        local = pl.ds(pl.multiple_of(i * 32, 32), 32)
        gain = gain1[...]
        _, slope = gelu_parts(n1[pl.ds(pl.multiple_of(i * 32 + 16, 16), 32), :] * gain)
        h1[local, :] = slope * gain

    load_cot.wait()
    arrived(got_cot)
    arrived(got_sq)
    spread(
        lax.rsqrt((sqs[0] + sqs[1] + sqs[2] + sqs[3]) * (1.0 / D2) + EPS), s2
    )
    g2acc[...] = jnp.zeros_like(g2acc)

    def second_norm(rows, cot, own, count):
        scale = s2[rows, :]
        scale = jnp.concatenate([scale, scale], axis=1)
        normed = c2[rows, :] * scale
        gain = gain2[...]
        pre = normed * gain
        cdf, slope = gelu_parts(pre)
        dpre = cot * slope
        dnormed = dpre * gain
        inner = dnormed * normed
        c2[rows, :] = normed
        dn2[rows, :] = dnormed
        q[rows, :] = inner[:, :128] + inner[:, 128:]
        if own is not None:
            feat_ref[own, :] = (pre * cdf).astype(BF16)
            g2acc[...] += jnp.sum(dpre * normed, axis=0, keepdims=True)

    second_norm(pl.ds(8, 8), cext[pl.ds(0, 16), :].astype(F32)[8:16], None, 8)
    second_norm(pl.ds(400, 8), cext[pl.ds(400, 16), :].astype(F32)[0:8], None, 8)

    @pl.loop(0, 8)
    def _(i):
        rows = pl.ds(pl.multiple_of(16 + i * 48, 16), 48)
        own = pl.ds(pl.multiple_of(i * 48, 16), 48)
        second_norm(rows, cext[rows, :].astype(F32), own, 48)

    got_in = row_sums(ins, S_IN)
    arrived(got_in)
    spread((ins[0] + ins[1] + ins[2] + ins[3]) * (1.0 / D2), m2)

    def rows_of(b):
        return pl.ds(pl.multiple_of(b * ROWS, 128), ROWS)

    def expand(b, half):
        for tap in range(KW2):
            for k in range(8):
                dcat[
                    pl.ds(pl.multiple_of(b * ROWS + 48 * k, 16), 48),
                    pl.ds(128 * (half * KW2 + tap), 128),
                ] = d2f[pl.ds(48 * k + 18 - tap, 48), :].astype(BF16)

    got_d2 = []
    for half in range(2):
        columns = pl.ds(128 * half, 128)
        d2[half, pl.ds(0, 8), :] = jnp.zeros((8, 128), F32)
        d2[half, pl.ds(408, 8), :] = jnp.zeros((8, 128), F32)
        for start, count in pieces:
            rows = pl.ds(start, count)
            grad = s2[rows, :] * (dn2[rows, columns] - c2[rows, columns] * m2[rows, :])
            if start == 8:
                grad = jnp.where(s > 0, grad, 0.0)
            if start == 400:
                grad = jnp.where(s < NS - 1, grad, 0.0)
            d2[half, rows, :] = grad
        d2s[x, half] = d2[half].astype(BF16)
        got_d2.append(
            [
                send(
                    d2s.at[x, half],
                    d2s.at[x, half],
                    S_D2 + 3 * half + k - 1,
                    (seq_of(y, x_peer(k), z), c),
                )
                for k in range(1, NX)
            ]
        )
    for half in range(2):
        d2f[...] = d2[half]
        expand(x, half)
    dact[...] = nt_dot(dcat[rows_of(x), :], w2v[...]).astype(BF16)
    g1acc[...] = jnp.zeros_like(g1acc)

    @pl.loop(0, ROWS // 32)
    def _(i):
        local = pl.ds(pl.multiple_of(i * 32, 32), 32)
        rows = pl.ds(pl.multiple_of(16 + i * 32, 16), 32)
        normed = n1[rows, :]
        dnormed = dact[local, :].astype(F32) * h1[local, :]
        inner = dnormed * normed
        g1acc[...] += jnp.sum(inner, axis=0, keepdims=True)
        mean = jnp.sum(inner, axis=1, keepdims=True) * (1.0 / D1)
        dc1[local, :] = (s1[rows, :][:, :1] * (dnormed - normed * mean)).astype(BF16)

    pay[...] = tn_dot(uu[pl.ds(16, ROWS), :], dc1[...])
    pay[pl.ds(60, 1), :] = g1acc[...] / gain1[...]
    for k in range(NC):
        chs[k, :, pl.ds(0, 128)] = pay[:, OWN1 * k : OWN1 * k + 128].astype(BF16)
        chs[k, :, pl.ds(128, 128)] = jnp.concatenate(
            [pay[:, OWN1 * k + 128 : OWN1 * k + 192], jnp.zeros((64, 64), F32)], axis=1
        ).astype(BF16)
    got_ch = [
        send(chs.at[c_peer(k)], chr_.at[c], S_CH + k - 1, (s, c_peer(k))) for k in (2, 1, 3)
    ]
    chr_[c] = chs[c]

    def add_up(slots, count):
        total = slots[0].astype(F32)
        for k in range(1, count):
            total = total + slots[k].astype(F32)
        return total

    def half_grad(half):
        arrived(got_d2[half])
        for k in range(1, NX):
            b = x_peer(k)
            d2f[...] = d2s[b, half].astype(F32)
            expand(b, half)
        columns = pl.ds(HALF * half, HALF)
        total = jnp.dot(aget[0], dcat[pl.ds(0, ROWS), columns], preferred_element_type=F32)
        for b in range(1, NX):
            total = total + jnp.dot(
                aget[b], dcat[pl.ds(ROWS * b, ROWS), columns], preferred_element_type=F32
            )
        part[...] = total
        for yy in range(NY):
            rows = pl.ds(24 * yy, 24)
            taps = [part[rows, pl.ds(128 * tap, 128)] for tap in range(KW2)]
            taps.append(jnp.zeros((8, 128), F32))
            for first in (0, 2, 4):
                piece = jnp.concatenate(taps[first : first + 2], axis=0).astype(BF16)
                big[half, yy, pl.ds(24 * first, piece.shape[0]), :] = piece

    def half_send(half):
        copies = [
            send(
                big.at[half, y_peer(k)],
                ryg.at[half, y],
                S_GY + 7 * half + k - 1,
                (seq_of(y_peer(k), x, z), c),
            )
            for k in (4, 3, 5, 2, 6, 1, 7)
        ]
        ryg[half, y] = big[half, y]
        return copies

    arrived(got_act)
    half_grad(0)
    got_y0 = half_send(0)
    arrived(got_ch)
    pay[:, pl.ds(0, 256)] = add_up(chr_, NC)
    pay[pl.ds(61, 1), pl.ds(0, 128)] = g2acc[:, :128]
    pay[pl.ds(62, 1), pl.ds(0, 128)] = g2acc[:, 128:]
    for k in range(NX):
        rsend[k] = pay[pl.ds(16 * k, 16), pl.ds(0, 256)].astype(BF16)
    got_rx = [
        send(rsend.at[x_peer(k)], rxs.at[x], S_RX + k - 1, (seq_of(y, x_peer(k), z), c))
        for k in range(1, NX)
    ]
    rxs[x] = rsend[x]
    half_grad(1)
    arrived(got_rx)
    rys[y] = add_up(rxs, NX).astype(BF16)
    got_ry = [
        send(rys.at[y], rys.at[y], S_RY + k - 1, (seq_of(y_peer(k), x, z), c)) for k in range(1, NY)
    ]
    got_y1 = half_send(1)

    def half_sum(half):
        total = ryg[half, 0].astype(F32)
        for k in range(1, NY):
            total = total + ryg[half, k].astype(F32)
        fin[half] = total

    arrived(got_ry)
    rzs[z] = add_up(rys, NY).astype(BF16)
    got_rz = [
        send(rzs.at[z], rzs.at[z], S_RZ + k - 1, (seq_of(y, x, z_peer(k)), c)) for k in range(1, NZ)
    ]
    arrived(got_y0)
    half_sum(0)
    arrived(got_rz)
    rgs[x] = add_up(rzs, NZ)
    got_rg = [
        send(rgs.at[x], rgs.at[x], S_RG + k - 1, (seq_of(y, x_peer(k), z), c)) for k in range(1, NX)
    ]
    arrived(got_y1)
    half_sum(1)
    for zz in range(NZ):
        for tap in range(KW2):
            rows = pl.ds(24 * tap + 6 * zz, 8)
            zsl[zz, pl.ds(16 * tap, 16), :] = jnp.concatenate(
                [fin[0, rows, :], fin[1, rows, :]], axis=0
            ).astype(BF16)
    got_z = [
        send(zsl.at[z_peer(k)], rzl.at[z], S_Z + k - 1, (seq_of(y, x, z_peer(k)), c))
        for k in range(1, NZ)
    ]
    rzl[z] = zsl[z]
    arrived(got_z)
    total = add_up(rzl, NZ)
    for tap in range(KW2):
        for half in range(2):
            gw2_ref[tap, :, pl.ds(128 * half, 128)] = total[16 * tap + 8 * half : 16 * tap + 8 * half + 6]
    arrived(got_rg)
    for k in range(NX):
        for j in range(4):
            tap = 4 * k + j
            if tap < KW1:
                gw1_ref[tap] = rgs[k, pl.ds(4 * j, 4), pl.ds(0, OWN1)]
    gg1_ref[...] = rgs[3, pl.ds(12, 1), pl.ds(0, OWN1)].reshape(OWN1)
    gg2_ref[...] = jnp.concatenate(
        [rgs[3, pl.ds(13, 1), pl.ds(0, 128)], rgs[3, pl.ds(14, 1), pl.ds(0, 128)]], axis=1
    ).reshape(OWN2)
    for copy in pending:
        copy.wait_send()


def write_out(*refs):
    copies = [pltpu.make_async_copy(refs[i], refs[5 + i], refs[10].at[i]) for i in range(5)]
    for copy in copies:
        copy.start()
    for copy in copies:
        copy.wait()


def on_device(bases, conv1_weight, gain1, conv2_weight, gain2, cotangent):
    vmem = pl.BlockSpec(memory_space=pltpu.VMEM)
    hbm = pl.BlockSpec(memory_space=pl.ANY)
    V = pltpu.VMEM
    results = pl.pallas_call(
        kernel,
        out_shape=(
            jax.ShapeDtypeStruct((ROWS, OWN2), BF16),
            jax.ShapeDtypeStruct((KW1, BASES, OWN1), F32),
            jax.ShapeDtypeStruct((OWN1,), F32),
            jax.ShapeDtypeStruct((KW2, 6, OWN2), F32),
            jax.ShapeDtypeStruct((OWN2,), F32),
        ),
        in_specs=[hbm] * 6,
        out_specs=(vmem,) * 5,
        scratch_shapes=[
            V((ROWS,), jnp.int32),
            V((OWN1,), F32),
            V((OWN2,), F32),
            V((1, 640), jnp.int32),
            V((FRAME, OWN2), BF16),
            V((NC, KW1, BASES, OWN1), BF16),
            V((NC, 1, OWN1), F32),
            V((1, D1), F32),
            V((1, OWN2), F32),
            V((64, D1), BF16),
            V((64, 512), F32),
            V((512, 64), BF16),
            V((FRAME, D1), F32),
            V((FRAME, 128), F32),
            V((ROWS, D1), F32),
            V((FRAME, D1), BF16),
            V((D1, ROWS), F32),
            V((NX, SHARE, ROWS), BF16),
            V((NX, SHARE, ROWS), BF16),
            V((D1, WIDE), BF16),
            V((FRAME, WIDE), F32),
            V((FRAME, OWN2), F32),
            V((FRAME, OWN2), F32),
            V((512, 128), F32),
            V((512, 128), F32),
            V((512, 128), F32),
            V((NC, 1, 512), F32),
            V((NC, 1, 512), F32),
            V((2, FRAME, 128), F32),
            V((NX, 2, FRAME, 128), BF16),
            V((FRAME, 128), F32),
            V((NX * ROWS, WIDE), BF16),
            V((1, OWN2), F32),
            V((1, D1), F32),
            V((ROWS, D1), BF16),
            V((ROWS, D1), BF16),
            V((64, D1), F32),
            V((NC, 64, 256), BF16),
            V((NC, 64, 256), BF16),
            V((NX, 16, 256), BF16),
            V((NX, 16, 256), BF16),
            V((NY, 16, 256), BF16),
            V((NZ, 16, 256), BF16),
            V((NX, 16, 256), F32),
            V((SHARE, HALF), F32),
            V((2, NY, 128, 128), BF16),
            V((2, NY, 128, 128), BF16),
            V((2, 128, 128), F32),
            V((NZ, 80, 128), BF16),
            V((NZ, 80, 128), BF16),
            pltpu.SemaphoreType.DMA((N_SEM,)),
            pltpu.SemaphoreType.DMA((N_SEM,)),
            pltpu.SemaphoreType.DMA((15,)),
        ],
        compiler_params=pltpu.CompilerParams(
            collective_id=0, has_side_effects=True, vmem_limit_bytes=58 * 1024 * 1024
        ),
        cost_estimate=pl.CostEstimate(
            flops=3 * 2 * ROWS * D1 * KW2 * OWN2, bytes_accessed=4 << 20, transcendentals=1 << 20
        ),
    )(
        bases,
        conv1_weight.transpose(1, 0, 2),
        gain1,
        conv2_weight.transpose(1, 0, 2),
        gain2,
        cotangent,
    )
    features, gw1, gg1, gw2, gg2 = pl.pallas_call(
        write_out,
        out_shape=tuple(jax.ShapeDtypeStruct(r.shape, r.dtype) for r in results),
        in_specs=[vmem] * 5,
        out_specs=(hbm,) * 5,
        scratch_shapes=[pltpu.SemaphoreType.DMA((5,))],
    )(*results)
    return (features, gw1.transpose(1, 0, 2), gg1, gw2.transpose(1, 0, 2), gg2)


def solution(mesh):
    in_specs = (
        P("seq"),
        P(None, None, "ch"),
        P("ch"),
        P(None, None, "ch"),
        P("ch"),
        P("seq", "ch"),
    )
    out_specs = (P("seq", "ch"), P(None, None, "ch"), P("ch"), P("seq", None, "ch"), P("ch"))
    return jax.shard_map(
        on_device, mesh=mesh, in_specs=in_specs, out_specs=out_specs, check_vma=False
    )
```

```python
import math

import jax
import jax.numpy as jnp
from jax import lax
from jax.experimental import pallas as pl
from jax.experimental.pallas import tpu as pltpu
from jax.sharding import PartitionSpec as P

BASES = 4
KW1 = 15
KW2 = 5
D1 = 768
D2 = 1024
OWN1 = 192
OWN2 = 256
ROWS = 384
FRAME = 416
NX, NY, NZ, NC = 4, 8, 4, 4
NS = NX * NY * NZ
TAPS1 = KW1 * BASES
WIDE = KW2 * OWN2
HALF = WIDE // 2
SHARE = D1 // NX
EPS = 1e-06
MESH = pl.DeviceIdType.MESH
F32 = jnp.float32
BF16 = jnp.bfloat16
ROOT = math.sqrt(2.0 / math.pi)

S_BASE, S_COT, S_W1, S_G1 = 0, 2, 4, 7
S_SQ, S_IN, S_CH = 10, 13, 16
S_ACT, S_D2 = 19, 22
S_RX, S_RY, S_RZ, S_RG = 28, 31, 38, 41
S_Y1, S_Z1, S_Z2, S_Y2 = 44, 58, 64, 70
N_SEM = 84


def gelu_parts(v):
    square = v * v
    t = jnp.tanh(ROOT * (v + 0.044715 * (square * v)))
    cdf = 0.5 * (1.0 + t)
    slope = cdf + (0.5 * ROOT) * v * (1.0 - t * t) * (1.0 + (3.0 * 0.044715) * square)
    return cdf, slope


def nt_dot(a, b):
    return lax.dot_general(a, b, (((1,), (1,)), ((), ())), preferred_element_type=F32)


def tn_dot(a, b):
    return lax.dot_general(a, b, (((0,), (0,)), ((), ())), preferred_element_type=F32)


def kernel(
    bases_hbm, w1_hbm, g1_hbm, w2_ref, g2_hbm, cot_ref,
    feat_ref, gw1_ref, gg1_ref, gw2_ref, gg2_ref,
    bases_ref, g1_ref, g2_ref, bext, cext, w1g, g1g, gain1, gain2, w1full, ut, uu, n1, s1, h1, act, actt, asel, aget,
    w2v, ybuf, c2, dn2, q, s2, m2, sqs, ins, d2, d2s, d2f, dcat, g2acc, g1acc,
    dact, dc1, pay, chs, chr_, rsend, rxs, rys, rzs, rgs,
    part, zpack, zbig, rz0, yb, ry0, big, ryg, fin, zfin, zsl, rzl,
    ssem, rsem, lsem,
):
    s = lax.axis_index("seq")
    c = lax.axis_index("ch")
    z = lax.rem(s, NZ)
    x = lax.rem(lax.div(s, NZ), NX)
    y = lax.div(s, NZ * NX)

    def seq_of(yy, xx, zz):
        return (yy * NX + xx) * NZ + zz

    def x_peer(k):
        return lax.rem(x + k, NX)

    def y_peer(k):
        return lax.rem(y + k, NY)

    def z_peer(k):
        return lax.rem(z + k, NZ)

    def c_peer(k):
        return lax.rem(c + k, NC)

    right = lax.rem(s + 1, NS)
    left = lax.rem(s + NS - 1, NS)

    first_loads = [
        pltpu.make_async_copy(bases_hbm, bases_ref, lsem.at[11]),
        pltpu.make_async_copy(w1_hbm, w1g.at[c], lsem.at[12]),
        pltpu.make_async_copy(g1_hbm, g1_ref, lsem.at[13]),
        pltpu.make_async_copy(g2_hbm, g2_ref, lsem.at[14]),
    ]
    for load in first_loads:
        load.start()
    loads = []
    for half in range(2):
        for tap in range(KW2):
            n = half * KW2 + tap
            loads.append(
                pltpu.make_async_copy(
                    w2_ref.at[tap, :, pl.ds(128 * half, 128)],
                    w2v.at[:, pl.ds(128 * n, 128)],
                    lsem.at[n],
                )
            )
    for load in loads:
        load.start()
    load_cot = pltpu.make_async_copy(cot_ref, cext.at[pl.ds(16, ROWS)], lsem.at[10])
    load_cot.start()

    barrier = pltpu.get_barrier_semaphore()
    friends = [(right, c), (left, c)]
    friends += [(s, c_peer(k)) for k in range(1, NC)]
    friends += [(seq_of(y, x_peer(k), z), c) for k in range(1, NX)]
    friends += [(seq_of(y_peer(k), x, z), c) for k in range(1, NY)]
    friends += [(seq_of(y, x, z_peer(k)), c) for k in range(1, NZ)]
    for friend in friends:
        pl.semaphore_signal(barrier, inc=1, device_id=friend, device_id_type=MESH)
    for load in first_loads:
        load.wait()
    bext[:, pl.ds(128, ROWS)] = bases_ref[...].reshape(1, ROWS)
    g1g[c] = g1_ref[...].reshape(1, OWN1)
    gain2[...] = g2_ref[...].reshape(1, OWN2)
    pl.semaphore_wait(barrier, len(friends))

    pending = []

    def send(src, dst, number, to):
        copy = pltpu.make_async_remote_copy(
            src_ref=src,
            dst_ref=dst,
            send_sem=ssem.at[number],
            recv_sem=rsem.at[number],
            device_id=to,
            device_id_type=MESH,
        )
        copy.start()
        pending.append(copy)
        return copy

    def arrived(copies):
        for copy in copies:
            copy.wait_recv()

    got_bases = [
        send(bext.at[:, pl.ds(384, 128)], bext.at[:, pl.ds(0, 128)], S_BASE, (right, c)),
        send(bext.at[:, pl.ds(128, 128)], bext.at[:, pl.ds(512, 128)], S_BASE + 1, (left, c)),
    ]
    got_w1 = []
    for k in (2, 1, 3):
        to = (s, c_peer(k))
        got_w1.append(send(w1g.at[c], w1g.at[c], S_W1 + k - 1, to))
        got_w1.append(send(g1g.at[c], g1g.at[c], S_G1 + k - 1, to))
    got_cot = [
        send(cot_ref.at[pl.ds(ROWS - 16, 16)], cext.at[pl.ds(0, 16)], S_COT, (right, c)),
        send(cot_ref.at[pl.ds(0, 16)], cext.at[pl.ds(16 + ROWS, 16)], S_COT + 1, (left, c)),
    ]

    arrived(got_bases)
    place = lax.broadcasted_iota(jnp.int32, (1, 640), 1) - 128 + s * ROWS
    known = jnp.where((place >= 0) & (place < NS * ROWS), bext[...], -1)
    kinds = lax.broadcasted_iota(jnp.int32, (BASES, 512), 0)
    for tap in range(KW1):
        rolled = pltpu.roll(known, 640 - (105 + tap), 1)[:, :512]
        ut[pl.ds(BASES * tap, BASES), :] = (
            jnp.broadcast_to(rolled, (BASES, 512)) == kinds
        ).astype(F32)
    ut[pl.ds(BASES * KW1, 4), :] = jnp.zeros((4, 512), F32)
    for block in range(4):
        uu[pl.ds(128 * block, 128), :] = ut[:, pl.ds(128 * block, 128)].T.astype(BF16)

    arrived(got_w1)
    w1full[pl.ds(0, TAPS1), :] = jnp.concatenate(
        [w1g[k].astype(F32).reshape(TAPS1, OWN1) for k in range(NC)], axis=1
    ).astype(BF16)
    w1full[pl.ds(TAPS1, 4), :] = jnp.zeros((4, D1), BF16)
    gain1[...] = jnp.concatenate([g1g[k] for k in range(NC)], axis=1)
    n1[...] = jnp.dot(uu[pl.ds(0, FRAME), :], w1full[...], preferred_element_type=F32)

    @pl.loop(0, FRAME // 32)
    def _(i):
        rows = pl.ds(pl.multiple_of(i * 32, 32), 32)
        v = n1[rows, :]
        scale = lax.rsqrt(jnp.sum(v * v, axis=1, keepdims=True) * (1.0 / D1) + EPS)
        normed = v * scale
        n1[rows, :] = normed
        s1[rows, :] = jnp.broadcast_to(scale, (32, 128))
        pre = normed * gain1[...]
        cdf, _ = gelu_parts(pre)
        where = lax.broadcasted_iota(jnp.int32, (32, 1), 0) + (i * 32 - 16) + s * ROWS
        inside = (where >= 0) & (where < NS * ROWS)
        act[rows, :] = jnp.where(inside, pre * cdf, 0.0).astype(BF16)

    for load in loads:
        load.wait()
    ybuf[...] = jnp.dot(act[...], w2v[...], preferred_element_type=F32)
    pieces = [(8, 8)] + [(16 + 48 * k, 48) for k in range(8)] + [(400, 8)]
    q[pl.ds(0, 8), :] = jnp.zeros((8, 128), F32)
    q[pl.ds(408, 104), :] = jnp.zeros((104, 128), F32)
    for start, count in pieces:
        squares = None
        for half in range(2):
            total = None
            for tap in range(KW2):
                term = ybuf[
                    pl.ds(start + tap - 2, count), pl.ds(128 * (half * KW2 + tap), 128)
                ]
                total = term if total is None else total + term
            c2[pl.ds(start, count), pl.ds(128 * half, 128)] = total
            squares = total * total if squares is None else squares + total * total
        q[pl.ds(start, count), :] = squares
    def row_sums(slots, number):
        for block in range(4):
            slots[c, :, pl.ds(128 * block, 128)] = jnp.sum(
                q[pl.ds(128 * block, 128), :].T, axis=0, keepdims=True
            )
        return [
            send(slots.at[c], slots.at[c], number + k - 1, (s, c_peer(k))) for k in (2, 1, 3)
        ]

    def spread(row, columns):
        for block in range(4):
            columns[pl.ds(128 * block, 128), :] = jnp.broadcast_to(
                row[:, 128 * block : 128 * block + 128], (128, 128)
            ).T

    got_sq = row_sums(sqs, S_SQ)
    for a in range(3):
        for b in range(6):
            tile = act[pl.ds(16 + 128 * a, 128), pl.ds(128 * b, 128)].astype(F32)
            actt[pl.ds(128 * b, 128), pl.ds(128 * a, 128)] = tile.T
    for xx in range(NX):
        for yy in range(0, NY, 2):
            asel[xx, pl.ds(24 * yy, 48), :] = jnp.concatenate(
                [
                    actt[pl.ds(96 * yy + 24 * xx, 24), :],
                    actt[pl.ds(96 * yy + 96 + 24 * xx, 24), :],
                ],
                axis=0,
            ).astype(BF16)
    got_act = [
        send(asel.at[x_peer(k)], aget.at[x], S_ACT + k - 1, (seq_of(y, x_peer(k), z), c))
        for k in range(1, NX)
    ]
    aget[x] = asel[x]

    @pl.loop(0, ROWS // 32)
    def _(i):
        local = pl.ds(pl.multiple_of(i * 32, 32), 32)
        gain = gain1[...]
        _, slope = gelu_parts(n1[pl.ds(pl.multiple_of(i * 32 + 16, 16), 32), :] * gain)
        h1[local, :] = slope * gain

    load_cot.wait()
    arrived(got_cot)
    arrived(got_sq)
    spread(
        lax.rsqrt((sqs[0] + sqs[1] + sqs[2] + sqs[3]) * (1.0 / D2) + EPS), s2
    )
    g2acc[...] = jnp.zeros_like(g2acc)

    def second_norm(rows, cot, own, count):
        scale = s2[rows, :]
        scale = jnp.concatenate([scale, scale], axis=1)
        normed = c2[rows, :] * scale
        gain = gain2[...]
        pre = normed * gain
        cdf, slope = gelu_parts(pre)
        dpre = cot * slope
        dnormed = dpre * gain
        inner = dnormed * normed
        c2[rows, :] = normed
        dn2[rows, :] = dnormed
        q[rows, :] = inner[:, :128] + inner[:, 128:]
        if own is not None:
            feat_ref[own, :] = (pre * cdf).astype(BF16)
            g2acc[...] += jnp.sum(dpre * normed, axis=0, keepdims=True)

    second_norm(pl.ds(8, 8), cext[pl.ds(0, 16), :].astype(F32)[8:16], None, 8)
    second_norm(pl.ds(400, 8), cext[pl.ds(400, 16), :].astype(F32)[0:8], None, 8)

    @pl.loop(0, 8)
    def _(i):
        rows = pl.ds(pl.multiple_of(16 + i * 48, 16), 48)
        own = pl.ds(pl.multiple_of(i * 48, 16), 48)
        second_norm(rows, cext[rows, :].astype(F32), own, 48)

    got_in = row_sums(ins, S_IN)
    arrived(got_in)
    spread((ins[0] + ins[1] + ins[2] + ins[3]) * (1.0 / D2), m2)

    def rows_of(b):
        return pl.ds(pl.multiple_of(b * ROWS, 128), ROWS)

    def expand(b, half):
        for tap in range(KW2):
            for k in range(8):
                dcat[
                    pl.ds(pl.multiple_of(b * ROWS + 48 * k, 16), 48),
                    pl.ds(128 * (half * KW2 + tap), 128),
                ] = d2f[pl.ds(48 * k + 18 - tap, 48), :].astype(BF16)

    got_d2 = []
    for half in range(2):
        columns = pl.ds(128 * half, 128)
        d2[half, pl.ds(0, 8), :] = jnp.zeros((8, 128), F32)
        d2[half, pl.ds(408, 8), :] = jnp.zeros((8, 128), F32)
        for start, count in pieces:
            rows = pl.ds(start, count)
            grad = s2[rows, :] * (dn2[rows, columns] - c2[rows, columns] * m2[rows, :])
            if start == 8:
                grad = jnp.where(s > 0, grad, 0.0)
            if start == 400:
                grad = jnp.where(s < NS - 1, grad, 0.0)
            d2[half, rows, :] = grad
        d2s[x, half] = d2[half].astype(BF16)
        got_d2.append(
            [
                send(
                    d2s.at[x, half],
                    d2s.at[x, half],
                    S_D2 + 3 * half + k - 1,
                    (seq_of(y, x_peer(k), z), c),
                )
                for k in range(1, NX)
            ]
        )
    for half in range(2):
        d2f[...] = d2[half]
        expand(x, half)
    dact[...] = nt_dot(dcat[rows_of(x), :], w2v[...]).astype(BF16)
    g1acc[...] = jnp.zeros_like(g1acc)

    @pl.loop(0, ROWS // 32)
    def _(i):
        local = pl.ds(pl.multiple_of(i * 32, 32), 32)
        rows = pl.ds(pl.multiple_of(16 + i * 32, 16), 32)
        normed = n1[rows, :]
        dnormed = dact[local, :].astype(F32) * h1[local, :]
        inner = dnormed * normed
        g1acc[...] += jnp.sum(inner, axis=0, keepdims=True)
        mean = jnp.sum(inner, axis=1, keepdims=True) * (1.0 / D1)
        dc1[local, :] = (s1[rows, :][:, :1] * (dnormed - normed * mean)).astype(BF16)

    pay[...] = tn_dot(uu[pl.ds(16, ROWS), :], dc1[...])
    pay[pl.ds(60, 1), :] = g1acc[...] / gain1[...]
    for k in range(NC):
        chs[k, :, pl.ds(0, 128)] = pay[:, OWN1 * k : OWN1 * k + 128].astype(BF16)
        chs[k, :, pl.ds(128, 128)] = jnp.concatenate(
            [pay[:, OWN1 * k + 128 : OWN1 * k + 192], jnp.zeros((64, 64), F32)], axis=1
        ).astype(BF16)
    got_ch = [
        send(chs.at[c_peer(k)], chr_.at[c], S_CH + k - 1, (s, c_peer(k))) for k in (2, 1, 3)
    ]
    chr_[c] = chs[c]

    def add_up(slots, count):
        total = slots[0].astype(F32)
        for k in range(1, count):
            total = total + slots[k].astype(F32)
        return total

    def half_grad(half):
        arrived(got_d2[half])
        for k in range(1, NX):
            b = x_peer(k)
            d2f[...] = d2s[b, half].astype(F32)
            expand(b, half)
        columns = pl.ds(HALF * half, HALF)
        total = jnp.dot(aget[0], dcat[pl.ds(0, ROWS), columns], preferred_element_type=F32)
        for b in range(1, NX):
            total = total + jnp.dot(
                aget[b], dcat[pl.ds(ROWS * b, ROWS), columns], preferred_element_type=F32
            )
        part[...] = total

    def pack(half):
        for yy in range(NY):
            rows = pl.ds(24 * yy, 24)
            taps = [part[rows, pl.ds(128 * tap, 128)] for tap in range(3)]
            big[half, yy, pl.ds(0, 48), :] = jnp.concatenate(taps[:2], axis=0).astype(BF16)
            big[half, yy, pl.ds(48, 32), :] = jnp.concatenate(
                [taps[2], jnp.zeros((8, 128), F32)], axis=0
            ).astype(BF16)
            for zz in range(NZ):
                for tap in (3, 4):
                    zpack[zz, yy, pl.ds(6 * tap - 18, 6), :] = part[
                        pl.ds(24 * yy + 6 * zz, 6), pl.ds(128 * tap, 128)
                    ]
        zpack[:, :, pl.ds(12, 4), :] = jnp.zeros((NZ, NY, 4, 128), F32)
        zbig[half] = zpack[...].astype(BF16)

    def y_sends(blocks, slots, half, number):
        copies = [
            send(
                blocks.at[half, y_peer(k)],
                slots.at[half, y],
                number + 7 * half + k - 1,
                (seq_of(y_peer(k), x, z), c),
            )
            for k in (4, 3, 5, 2, 6, 1, 7)
        ]
        slots[half, y] = blocks[half, y]
        return copies

    def z_sends(blocks, slots, half, number):
        copies = [
            send(
                blocks.at[half, z_peer(k)],
                slots.at[half, z],
                number + 3 * half + k - 1,
                (seq_of(y, x, z_peer(k)), c),
            )
            for k in (2, 1, 3)
        ]
        slots[half, z] = blocks[half, z]
        return copies

    def add_half(slots, half, count):
        total = slots[half, 0].astype(F32)
        for k in range(1, count):
            total = total + slots[half, k].astype(F32)
        return total

    def first_stage(half):
        return y_sends(big, ryg, half, S_Y1), z_sends(zbig, rz0, half, S_Z1)

    def second_stage(half, got):
        arrived(got[1])
        yb[half] = add_half(rz0, half, NZ).astype(BF16)
        over_y = y_sends(yb, ry0, half, S_Y2)
        arrived(got[0])
        fin[...] = add_half(ryg, half, NY)
        for zz in range(NZ):
            for tap in range(3):
                zfin[zz, pl.ds(6 * tap, 6), :] = fin[pl.ds(24 * tap + 6 * zz, 6), :]
            zfin[zz, pl.ds(18, 14), :] = jnp.zeros((14, 128), F32)
        zsl[half] = zfin[...].astype(BF16)
        return over_y, z_sends(zsl, rzl, half, S_Z2)

    def last_stage(half, got):
        columns = pl.ds(128 * half, 128)
        arrived(got[0])
        total = add_half(ry0, half, NY)
        for tap in (3, 4):
            gw2_ref[tap, :, columns] = total[6 * tap - 18 : 6 * tap - 12]
        arrived(got[1])
        total = add_half(rzl, half, NZ)
        for tap in range(3):
            gw2_ref[tap, :, columns] = total[6 * tap : 6 * tap + 6]

    arrived(got_act)
    half_grad(0)
    pack(0)
    first0 = first_stage(0)
    arrived(got_ch)
    pay[:, pl.ds(0, 256)] = add_up(chr_, NC)
    pay[pl.ds(61, 1), pl.ds(0, 128)] = g2acc[:, :128]
    pay[pl.ds(62, 1), pl.ds(0, 128)] = g2acc[:, 128:]
    for k in range(NX):
        rsend[k] = pay[pl.ds(16 * k, 16), pl.ds(0, 256)].astype(BF16)
    got_rx = [
        send(rsend.at[x_peer(k)], rxs.at[x], S_RX + k - 1, (seq_of(y, x_peer(k), z), c))
        for k in range(1, NX)
    ]
    rxs[x] = rsend[x]
    arrived(got_rx)
    rys[y] = add_up(rxs, NX).astype(BF16)
    got_ry = [
        send(rys.at[y], rys.at[y], S_RY + k - 1, (seq_of(y_peer(k), x, z), c))
        for k in (4, 3, 5, 2, 6, 1, 7)
    ]
    half_grad(1)
    pack(1)
    first1 = first_stage(1)
    second0 = second_stage(0, first0)
    arrived(got_ry)
    rzs[z] = add_up(rys, NY).astype(BF16)
    got_rz = [
        send(rzs.at[z], rzs.at[z], S_RZ + k - 1, (seq_of(y, x, z_peer(k)), c)) for k in range(1, NZ)
    ]
    second1 = second_stage(1, first1)
    arrived(got_rz)
    rgs[x] = add_up(rzs, NZ)
    got_rg = [
        send(rgs.at[x], rgs.at[x], S_RG + k - 1, (seq_of(y, x_peer(k), z), c)) for k in range(1, NX)
    ]
    last_stage(0, second0)
    last_stage(1, second1)
    arrived(got_rg)
    for k in range(NX):
        for j in range(4):
            tap = 4 * k + j
            if tap < KW1:
                gw1_ref[tap] = rgs[k, pl.ds(4 * j, 4), pl.ds(0, OWN1)]
    gg1_ref[...] = rgs[3, pl.ds(12, 1), pl.ds(0, OWN1)].reshape(OWN1)
    gg2_ref[...] = jnp.concatenate(
        [rgs[3, pl.ds(13, 1), pl.ds(0, 128)], rgs[3, pl.ds(14, 1), pl.ds(0, 128)]], axis=1
    ).reshape(OWN2)
    for copy in pending:
        copy.wait_send()


def write_out(*refs):
    copies = [pltpu.make_async_copy(refs[i], refs[5 + i], refs[10].at[i]) for i in range(5)]
    for copy in copies:
        copy.start()
    for copy in copies:
        copy.wait()


def on_device(bases, conv1_weight, gain1, conv2_weight, gain2, cotangent):
    vmem = pl.BlockSpec(memory_space=pltpu.VMEM)
    hbm = pl.BlockSpec(memory_space=pl.ANY)
    V = pltpu.VMEM
    results = pl.pallas_call(
        kernel,
        out_shape=(
            jax.ShapeDtypeStruct((ROWS, OWN2), BF16),
            jax.ShapeDtypeStruct((KW1, BASES, OWN1), F32),
            jax.ShapeDtypeStruct((OWN1,), F32),
            jax.ShapeDtypeStruct((KW2, 6, OWN2), F32),
            jax.ShapeDtypeStruct((OWN2,), F32),
        ),
        in_specs=[hbm] * 6,
        out_specs=(vmem,) * 5,
        scratch_shapes=[
            V((ROWS,), jnp.int32),
            V((OWN1,), F32),
            V((OWN2,), F32),
            V((1, 640), jnp.int32),
            V((FRAME, OWN2), BF16),
            V((NC, KW1, BASES, OWN1), BF16),
            V((NC, 1, OWN1), F32),
            V((1, D1), F32),
            V((1, OWN2), F32),
            V((64, D1), BF16),
            V((64, 512), F32),
            V((512, 64), BF16),
            V((FRAME, D1), F32),
            V((FRAME, 128), F32),
            V((ROWS, D1), F32),
            V((FRAME, D1), BF16),
            V((D1, ROWS), F32),
            V((NX, SHARE, ROWS), BF16),
            V((NX, SHARE, ROWS), BF16),
            V((D1, WIDE), BF16),
            V((FRAME, WIDE), F32),
            V((FRAME, OWN2), F32),
            V((FRAME, OWN2), F32),
            V((512, 128), F32),
            V((512, 128), F32),
            V((512, 128), F32),
            V((NC, 1, 512), F32),
            V((NC, 1, 512), F32),
            V((2, FRAME, 128), F32),
            V((NX, 2, FRAME, 128), BF16),
            V((FRAME, 128), F32),
            V((NX * ROWS, WIDE), BF16),
            V((1, OWN2), F32),
            V((1, D1), F32),
            V((ROWS, D1), BF16),
            V((ROWS, D1), BF16),
            V((64, D1), F32),
            V((NC, 64, 256), BF16),
            V((NC, 64, 256), BF16),
            V((NX, 16, 256), BF16),
            V((NX, 16, 256), BF16),
            V((NY, 16, 256), BF16),
            V((NZ, 16, 256), BF16),
            V((NX, 16, 256), F32),
            V((SHARE, HALF), F32),
            V((NZ, NY, 16, 128), F32),
            V((2, NZ, NY, 16, 128), BF16),
            V((2, NZ, NY, 16, 128), BF16),
            V((2, NY, 16, 128), BF16),
            V((2, NY, 16, 128), BF16),
            V((2, NY, 80, 128), BF16),
            V((2, NY, 80, 128), BF16),
            V((80, 128), F32),
            V((NZ, 32, 128), F32),
            V((2, NZ, 32, 128), BF16),
            V((2, NZ, 32, 128), BF16),
            pltpu.SemaphoreType.DMA((N_SEM,)),
            pltpu.SemaphoreType.DMA((N_SEM,)),
            pltpu.SemaphoreType.DMA((15,)),
        ],
        compiler_params=pltpu.CompilerParams(
            collective_id=0, has_side_effects=True, vmem_limit_bytes=58 * 1024 * 1024
        ),
        cost_estimate=pl.CostEstimate(
            flops=3 * 2 * ROWS * D1 * KW2 * OWN2, bytes_accessed=4 << 20, transcendentals=1 << 20
        ),
    )(
        bases,
        conv1_weight.transpose(1, 0, 2),
        gain1,
        conv2_weight.transpose(1, 0, 2),
        gain2,
        cotangent,
    )
    features, gw1, gg1, gw2, gg2 = pl.pallas_call(
        write_out,
        out_shape=tuple(jax.ShapeDtypeStruct(r.shape, r.dtype) for r in results),
        in_specs=[vmem] * 5,
        out_specs=(hbm,) * 5,
        scratch_shapes=[pltpu.SemaphoreType.DMA((5,))],
    )(*results)
    return (features, gw1.transpose(1, 0, 2), gg1, gw2.transpose(1, 0, 2), gg2)


def solution(mesh):
    in_specs = (
        P("seq"),
        P(None, None, "ch"),
        P("ch"),
        P(None, None, "ch"),
        P("ch"),
        P("seq", "ch"),
    )
    out_specs = (P("seq", "ch"), P(None, None, "ch"), P("ch"), P("seq", None, "ch"), P("ch"))
    return jax.shard_map(
        on_device, mesh=mesh, in_specs=in_specs, out_specs=out_specs, check_vma=False
    )
```

```python
import math

import jax
import jax.numpy as jnp
from jax import lax
from jax.experimental import pallas as pl
from jax.experimental.pallas import tpu as pltpu
from jax.sharding import PartitionSpec as P

BASES = 4
KW1 = 15
KW2 = 5
D1 = 768
D2 = 1024
OWN1 = 192
OWN2 = 256
ROWS = 384
FRAME = 416
NX, NY, NZ, NC = 4, 8, 4, 4
NS = NX * NY * NZ
TAPS1 = KW1 * BASES
WIDE = KW2 * OWN2
HALF = WIDE // 2
SHARE = D1 // NX
EPS = 1e-06
MESH = pl.DeviceIdType.MESH
F32 = jnp.float32
BF16 = jnp.bfloat16
ROOT = math.sqrt(2.0 / math.pi)

S_BASE, S_COT, S_W1, S_G1 = 0, 2, 4, 7
S_SQ, S_IN, S_CH = 10, 13, 16
S_ACT, S_D2 = 19, 22
S_RX, S_RY, S_RZ, S_RG = 28, 31, 38, 41
S_Y1, S_Z1, S_Z2, S_Y2 = 44, 58, 64, 70
N_SEM = 84


def gelu_parts(v):
    square = v * v
    t = jnp.tanh(ROOT * (v + 0.044715 * (square * v)))
    cdf = 0.5 * (1.0 + t)
    slope = cdf + (0.5 * ROOT) * v * (1.0 - t * t) * (1.0 + (3.0 * 0.044715) * square)
    return cdf, slope


def nt_dot(a, b):
    return lax.dot_general(a, b, (((1,), (1,)), ((), ())), preferred_element_type=F32)


def tn_dot(a, b):
    return lax.dot_general(a, b, (((0,), (0,)), ((), ())), preferred_element_type=F32)


def kernel(
    bases_hbm, w1_hbm, g1_hbm, w2_ref, g2_hbm, cot_ref,
    feat_ref, gw1_ref, gg1_ref, gw2_ref, gg2_ref,
    bases_ref, g1_ref, g2_ref, bext, cext, w1g, g1g, gain1, gain2, w1full, ut, uu, n1, s1, h1, act, actt, asel, aget,
    w2v, ybuf, c2, dn2, q, s2, m2, sqs, ins, d2, d2s, d2f, dcat, g2acc, g1acc,
    dact, dc1, pay, chs, chr_, rsend, rxs, rys, rzs, rgs,
    part, zpack, zbig, rz0, yb, ry0, big, ryg, fin, zfin, zsl, rzl,
    ssem, rsem, lsem,
):
    s = lax.axis_index("seq")
    c = lax.axis_index("ch")
    z = lax.rem(s, NZ)
    x = lax.rem(lax.div(s, NZ), NX)
    y = lax.div(s, NZ * NX)

    def seq_of(yy, xx, zz):
        return (yy * NX + xx) * NZ + zz

    def x_peer(k):
        return lax.rem(x + k, NX)

    def y_peer(k):
        return lax.rem(y + k, NY)

    def z_peer(k):
        return lax.rem(z + k, NZ)

    def c_peer(k):
        return lax.rem(c + k, NC)

    right = lax.rem(s + 1, NS)
    left = lax.rem(s + NS - 1, NS)

    first_loads = [
        pltpu.make_async_copy(bases_hbm, bases_ref, lsem.at[11]),
        pltpu.make_async_copy(w1_hbm, w1g.at[c], lsem.at[12]),
        pltpu.make_async_copy(g1_hbm, g1_ref, lsem.at[13]),
        pltpu.make_async_copy(g2_hbm, g2_ref, lsem.at[14]),
    ]
    for load in first_loads:
        load.start()
    loads = []
    for half in range(2):
        for tap in range(KW2):
            n = half * KW2 + tap
            loads.append(
                pltpu.make_async_copy(
                    w2_ref.at[tap, :, pl.ds(128 * half, 128)],
                    w2v.at[:, pl.ds(128 * n, 128)],
                    lsem.at[n],
                )
            )
    for load in loads:
        load.start()
    load_cot = pltpu.make_async_copy(cot_ref, cext.at[pl.ds(16, ROWS)], lsem.at[10])
    load_cot.start()

    barrier = pltpu.get_barrier_semaphore()
    friends = [(right, c), (left, c)]
    friends += [(s, c_peer(k)) for k in range(1, NC)]
    friends += [(seq_of(y, x_peer(k), z), c) for k in range(1, NX)]
    friends += [(seq_of(y_peer(k), x, z), c) for k in range(1, NY)]
    friends += [(seq_of(y, x, z_peer(k)), c) for k in range(1, NZ)]
    for friend in friends:
        pl.semaphore_signal(barrier, inc=1, device_id=friend, device_id_type=MESH)
    for load in first_loads:
        load.wait()
    bext[:, pl.ds(128, ROWS)] = bases_ref[...].reshape(1, ROWS)
    g1g[c] = g1_ref[...].reshape(1, OWN1)
    gain2[...] = g2_ref[...].reshape(1, OWN2)
    pl.semaphore_wait(barrier, len(friends))

    pending = []

    def send(src, dst, number, to):
        copy = pltpu.make_async_remote_copy(
            src_ref=src,
            dst_ref=dst,
            send_sem=ssem.at[number],
            recv_sem=rsem.at[number],
            device_id=to,
            device_id_type=MESH,
        )
        copy.start()
        pending.append(copy)
        return copy

    def arrived(copies):
        for copy in copies:
            copy.wait_recv()

    got_bases = [
        send(bext.at[:, pl.ds(384, 128)], bext.at[:, pl.ds(0, 128)], S_BASE, (right, c)),
        send(bext.at[:, pl.ds(128, 128)], bext.at[:, pl.ds(512, 128)], S_BASE + 1, (left, c)),
    ]
    got_w1 = []
    for k in (2, 1, 3):
        to = (s, c_peer(k))
        got_w1.append(send(w1g.at[c], w1g.at[c], S_W1 + k - 1, to))
        got_w1.append(send(g1g.at[c], g1g.at[c], S_G1 + k - 1, to))
    got_cot = [
        send(cot_ref.at[pl.ds(ROWS - 16, 16)], cext.at[pl.ds(0, 16)], S_COT, (right, c)),
        send(cot_ref.at[pl.ds(0, 16)], cext.at[pl.ds(16 + ROWS, 16)], S_COT + 1, (left, c)),
    ]

    arrived(got_bases)
    place = lax.broadcasted_iota(jnp.int32, (1, 640), 1) - 128 + s * ROWS
    known = jnp.where((place >= 0) & (place < NS * ROWS), bext[...], -1)
    kinds = lax.broadcasted_iota(jnp.int32, (BASES, 512), 0)
    for tap in range(KW1):
        rolled = pltpu.roll(known, 640 - (105 + tap), 1)[:, :512]
        ut[pl.ds(BASES * tap, BASES), :] = (
            jnp.broadcast_to(rolled, (BASES, 512)) == kinds
        ).astype(F32)
    ut[pl.ds(BASES * KW1, 4), :] = jnp.zeros((4, 512), F32)
    for block in range(4):
        uu[pl.ds(128 * block, 128), :] = ut[:, pl.ds(128 * block, 128)].T.astype(BF16)

    arrived(got_w1)
    w1full[pl.ds(0, TAPS1), :] = jnp.concatenate(
        [w1g[k].astype(F32).reshape(TAPS1, OWN1) for k in range(NC)], axis=1
    ).astype(BF16)
    w1full[pl.ds(TAPS1, 4), :] = jnp.zeros((4, D1), BF16)
    gain1[...] = jnp.concatenate([g1g[k] for k in range(NC)], axis=1)
    n1[...] = jnp.dot(uu[pl.ds(0, FRAME), :], w1full[...], preferred_element_type=F32)

    @pl.loop(0, FRAME // 32)
    def _(i):
        rows = pl.ds(pl.multiple_of(i * 32, 32), 32)
        v = n1[rows, :]
        scale = lax.rsqrt(jnp.sum(v * v, axis=1, keepdims=True) * (1.0 / D1) + EPS)
        normed = v * scale
        n1[rows, :] = normed
        s1[rows, :] = jnp.broadcast_to(scale, (32, 128))
        pre = normed * gain1[...]
        cdf, _ = gelu_parts(pre)
        where = lax.broadcasted_iota(jnp.int32, (32, 1), 0) + (i * 32 - 16) + s * ROWS
        inside = (where >= 0) & (where < NS * ROWS)
        act[rows, :] = jnp.where(inside, pre * cdf, 0.0).astype(BF16)

    for load in loads:
        load.wait()
    ybuf[...] = jnp.dot(act[...], w2v[...], preferred_element_type=F32)
    pieces = [(8, 8)] + [(16 + 48 * k, 48) for k in range(8)] + [(400, 8)]
    q[pl.ds(0, 8), :] = jnp.zeros((8, 128), F32)
    q[pl.ds(408, 104), :] = jnp.zeros((104, 128), F32)
    for start, count in pieces:
        squares = None
        for half in range(2):
            total = None
            for tap in range(KW2):
                term = ybuf[
                    pl.ds(start + tap - 2, count), pl.ds(128 * (half * KW2 + tap), 128)
                ]
                total = term if total is None else total + term
            c2[pl.ds(start, count), pl.ds(128 * half, 128)] = total
            squares = total * total if squares is None else squares + total * total
        q[pl.ds(start, count), :] = squares
    def row_sums(slots, number):
        for block in range(4):
            slots[c, :, pl.ds(128 * block, 128)] = jnp.sum(
                q[pl.ds(128 * block, 128), :].T, axis=0, keepdims=True
            )
        return [
            send(slots.at[c], slots.at[c], number + k - 1, (s, c_peer(k))) for k in (2, 1, 3)
        ]

    def spread(row, columns):
        for block in range(4):
            columns[pl.ds(128 * block, 128), :] = jnp.broadcast_to(
                row[:, 128 * block : 128 * block + 128], (128, 128)
            ).T

    got_sq = row_sums(sqs, S_SQ)
    for a in range(3):
        for b in range(6):
            tile = act[pl.ds(16 + 128 * a, 128), pl.ds(128 * b, 128)].astype(F32)
            actt[pl.ds(128 * b, 128), pl.ds(128 * a, 128)] = tile.T
    for xx in range(NX):
        for yy in range(0, NY, 2):
            asel[xx, pl.ds(24 * yy, 48), :] = jnp.concatenate(
                [
                    actt[pl.ds(96 * yy + 24 * xx, 24), :],
                    actt[pl.ds(96 * yy + 96 + 24 * xx, 24), :],
                ],
                axis=0,
            ).astype(BF16)
    got_act = [
        send(asel.at[x_peer(k)], aget.at[x], S_ACT + k - 1, (seq_of(y, x_peer(k), z), c))
        for k in range(1, NX)
    ]
    aget[x] = asel[x]

    @pl.loop(0, ROWS // 32)
    def _(i):
        local = pl.ds(pl.multiple_of(i * 32, 32), 32)
        gain = gain1[...]
        _, slope = gelu_parts(n1[pl.ds(pl.multiple_of(i * 32 + 16, 16), 32), :] * gain)
        h1[local, :] = slope * gain

    load_cot.wait()
    arrived(got_cot)
    arrived(got_sq)
    spread(
        lax.rsqrt((sqs[0] + sqs[1] + sqs[2] + sqs[3]) * (1.0 / D2) + EPS), s2
    )
    g2acc[...] = jnp.zeros_like(g2acc)

    def second_norm(rows, cot, own, count):
        scale = s2[rows, :]
        scale = jnp.concatenate([scale, scale], axis=1)
        normed = c2[rows, :] * scale
        gain = gain2[...]
        pre = normed * gain
        cdf, slope = gelu_parts(pre)
        dpre = cot * slope
        dnormed = dpre * gain
        inner = dnormed * normed
        c2[rows, :] = normed
        dn2[rows, :] = dnormed
        q[rows, :] = inner[:, :128] + inner[:, 128:]
        if own is not None:
            feat_ref[own, :] = (pre * cdf).astype(BF16)
            g2acc[...] += jnp.sum(dpre * normed, axis=0, keepdims=True)

    second_norm(pl.ds(8, 8), cext[pl.ds(0, 16), :].astype(F32)[8:16], None, 8)
    second_norm(pl.ds(400, 8), cext[pl.ds(400, 16), :].astype(F32)[0:8], None, 8)

    @pl.loop(0, 8)
    def _(i):
        rows = pl.ds(pl.multiple_of(16 + i * 48, 16), 48)
        own = pl.ds(pl.multiple_of(i * 48, 16), 48)
        second_norm(rows, cext[rows, :].astype(F32), own, 48)

    got_in = row_sums(ins, S_IN)
    arrived(got_in)
    spread((ins[0] + ins[1] + ins[2] + ins[3]) * (1.0 / D2), m2)

    def rows_of(b):
        return pl.ds(pl.multiple_of(b * ROWS, 128), ROWS)

    def expand(b, half):
        for tap in range(KW2):
            for k in range(8):
                dcat[
                    pl.ds(pl.multiple_of(b * ROWS + 48 * k, 16), 48),
                    pl.ds(128 * (half * KW2 + tap), 128),
                ] = d2f[pl.ds(48 * k + 18 - tap, 48), :].astype(BF16)

    got_d2 = []
    for half in range(2):
        columns = pl.ds(128 * half, 128)
        d2[half, pl.ds(0, 8), :] = jnp.zeros((8, 128), F32)
        d2[half, pl.ds(408, 8), :] = jnp.zeros((8, 128), F32)
        for start, count in pieces:
            rows = pl.ds(start, count)
            grad = s2[rows, :] * (dn2[rows, columns] - c2[rows, columns] * m2[rows, :])
            if start == 8:
                grad = jnp.where(s > 0, grad, 0.0)
            if start == 400:
                grad = jnp.where(s < NS - 1, grad, 0.0)
            d2[half, rows, :] = grad
        d2s[x, half] = d2[half].astype(BF16)
        got_d2.append(
            [
                send(
                    d2s.at[x, half],
                    d2s.at[x, half],
                    S_D2 + 3 * half + k - 1,
                    (seq_of(y, x_peer(k), z), c),
                )
                for k in range(1, NX)
            ]
        )
    for half in range(2):
        d2f[...] = d2[half]
        expand(x, half)
    dact[...] = nt_dot(dcat[rows_of(x), :], w2v[...]).astype(BF16)
    g1acc[...] = jnp.zeros_like(g1acc)

    @pl.loop(0, ROWS // 32)
    def _(i):
        local = pl.ds(pl.multiple_of(i * 32, 32), 32)
        rows = pl.ds(pl.multiple_of(16 + i * 32, 16), 32)
        normed = n1[rows, :]
        dnormed = dact[local, :].astype(F32) * h1[local, :]
        inner = dnormed * normed
        g1acc[...] += jnp.sum(inner, axis=0, keepdims=True)
        mean = jnp.sum(inner, axis=1, keepdims=True) * (1.0 / D1)
        dc1[local, :] = (s1[rows, :][:, :1] * (dnormed - normed * mean)).astype(BF16)

    pay[...] = tn_dot(uu[pl.ds(16, ROWS), :], dc1[...])
    pay[pl.ds(60, 1), :] = g1acc[...] / gain1[...]
    for k in range(NC):
        chs[k, pl.ds(0, 64), :] = pay[:, OWN1 * k : OWN1 * k + 128].astype(BF16)
        rest = pay[:, OWN1 * k + 128 : OWN1 * k + 192]
        chs[k, pl.ds(64, 32), :] = jnp.concatenate([rest[:32], rest[32:]], axis=1).astype(BF16)
    got_ch = [
        send(chs.at[c_peer(k)], chr_.at[c], S_CH + k - 1, (s, c_peer(k))) for k in (2, 1, 3)
    ]
    chr_[c] = chs[c]

    def add_up(slots, count):
        total = slots[0].astype(F32)
        for k in range(1, count):
            total = total + slots[k].astype(F32)
        return total

    def half_grad(half):
        arrived(got_d2[half])
        for k in range(1, NX):
            b = x_peer(k)
            d2f[...] = d2s[b, half].astype(F32)
            expand(b, half)
        columns = pl.ds(HALF * half, HALF)
        total = jnp.dot(aget[0], dcat[pl.ds(0, ROWS), columns], preferred_element_type=F32)
        for b in range(1, NX):
            total = total + jnp.dot(
                aget[b], dcat[pl.ds(ROWS * b, ROWS), columns], preferred_element_type=F32
            )
        part[...] = total

    def pack(half):
        for yy in range(NY):
            rows = pl.ds(24 * yy, 24)
            taps = [part[rows, pl.ds(128 * tap, 128)] for tap in range(3)]
            big[half, yy, pl.ds(0, 48), :] = jnp.concatenate(taps[:2], axis=0).astype(BF16)
            big[half, yy, pl.ds(48, 32), :] = jnp.concatenate(
                [taps[2], jnp.zeros((8, 128), F32)], axis=0
            ).astype(BF16)
            for zz in range(NZ):
                for tap in (3, 4):
                    zpack[zz, yy, pl.ds(6 * tap - 18, 6), :] = part[
                        pl.ds(24 * yy + 6 * zz, 6), pl.ds(128 * tap, 128)
                    ]
        zpack[:, :, pl.ds(12, 4), :] = jnp.zeros((NZ, NY, 4, 128), F32)
        zbig[half] = zpack[...].astype(BF16)

    def y_sends(blocks, slots, half, number):
        copies = [
            send(
                blocks.at[half, y_peer(k)],
                slots.at[half, y],
                number + 7 * half + k - 1,
                (seq_of(y_peer(k), x, z), c),
            )
            for k in (4, 3, 5, 2, 6, 1, 7)
        ]
        slots[half, y] = blocks[half, y]
        return copies

    def z_sends(blocks, slots, half, number):
        copies = [
            send(
                blocks.at[half, z_peer(k)],
                slots.at[half, z],
                number + 3 * half + k - 1,
                (seq_of(y, x, z_peer(k)), c),
            )
            for k in (2, 1, 3)
        ]
        slots[half, z] = blocks[half, z]
        return copies

    def add_half(slots, half, count):
        total = slots[half, 0].astype(F32)
        for k in range(1, count):
            total = total + slots[half, k].astype(F32)
        return total

    def first_stage(half):
        return y_sends(big, ryg, half, S_Y1), z_sends(zbig, rz0, half, S_Z1)

    def second_stage(half, got, between):
        arrived(got[1])
        yb[half] = add_half(rz0, half, NZ).astype(BF16)
        over_y = y_sends(yb, ry0, half, S_Y2)
        middle = between()
        arrived(got[0])
        fin[...] = add_half(ryg, half, NY)
        for zz in range(NZ):
            for tap in range(3):
                zfin[zz, pl.ds(6 * tap, 6), :] = fin[pl.ds(24 * tap + 6 * zz, 6), :]
            zfin[zz, pl.ds(18, 14), :] = jnp.zeros((14, 128), F32)
        zsl[half] = zfin[...].astype(BF16)
        return over_y, z_sends(zsl, rzl, half, S_Z2), middle

    def last_stage(half, got):
        columns = pl.ds(128 * half, 128)
        arrived(got[0])
        total = add_half(ry0, half, NY)
        for tap in (3, 4):
            gw2_ref[tap, :, columns] = total[6 * tap - 18 : 6 * tap - 12]
        arrived(got[1])
        total = add_half(rzl, half, NZ)
        for tap in range(3):
            gw2_ref[tap, :, columns] = total[6 * tap : 6 * tap + 6]

    arrived(got_act)
    half_grad(0)
    pack(0)
    first0 = first_stage(0)
    arrived(got_ch)
    small = add_up(chr_, NC)
    rest = small[64:]
    pay[:, pl.ds(0, 128)] = small[:64]
    pay[pl.ds(0, 32), pl.ds(128, 128)] = rest
    pay[pl.ds(32, 32), pl.ds(128, 128)] = jnp.concatenate([rest[:, 64:], rest[:, :64]], axis=1)
    pay[pl.ds(61, 1), pl.ds(0, 128)] = g2acc[:, :128]
    pay[pl.ds(62, 1), pl.ds(0, 128)] = g2acc[:, 128:]
    for k in range(NX):
        rsend[k] = pay[pl.ds(16 * k, 16), pl.ds(0, 256)].astype(BF16)
    got_rx = [
        send(rsend.at[x_peer(k)], rxs.at[x], S_RX + k - 1, (seq_of(y, x_peer(k), z), c))
        for k in range(1, NX)
    ]
    rxs[x] = rsend[x]
    arrived(got_rx)
    rys[y] = add_up(rxs, NX).astype(BF16)
    got_ry = [
        send(rys.at[y], rys.at[y], S_RY + k - 1, (seq_of(y_peer(k), x, z), c))
        for k in (4, 3, 5, 2, 6, 1, 7)
    ]
    half_grad(1)
    pack(1)
    first1 = first_stage(1)
    second0 = second_stage(0, first0, lambda: None)
    arrived(got_ry)
    rzs[z] = add_up(rys, NY).astype(BF16)
    got_rz = [
        send(rzs.at[z], rzs.at[z], S_RZ + k - 1, (seq_of(y, x, z_peer(k)), c)) for k in range(1, NZ)
    ]

    def gather_small():
        arrived(got_rz)
        rgs[x] = add_up(rzs, NZ)
        return [
            send(rgs.at[x], rgs.at[x], S_RG + k - 1, (seq_of(y, x_peer(k), z), c))
            for k in range(1, NX)
        ]

    second1 = second_stage(1, first1, gather_small)
    got_rg = second1[2]
    last_stage(0, second0)
    last_stage(1, second1)
    arrived(got_rg)
    for k in range(NX):
        for j in range(4):
            tap = 4 * k + j
            if tap < KW1:
                gw1_ref[tap] = rgs[k, pl.ds(4 * j, 4), pl.ds(0, OWN1)]
    gg1_ref[...] = rgs[3, pl.ds(12, 1), pl.ds(0, OWN1)].reshape(OWN1)
    gg2_ref[...] = jnp.concatenate(
        [rgs[3, pl.ds(13, 1), pl.ds(0, 128)], rgs[3, pl.ds(14, 1), pl.ds(0, 128)]], axis=1
    ).reshape(OWN2)
    for copy in pending:
        copy.wait_send()


def write_out(*refs):
    copies = [pltpu.make_async_copy(refs[i], refs[5 + i], refs[10].at[i]) for i in range(5)]
    for copy in copies:
        copy.start()
    for copy in copies:
        copy.wait()


def on_device(bases, conv1_weight, gain1, conv2_weight, gain2, cotangent):
    vmem = pl.BlockSpec(memory_space=pltpu.VMEM)
    hbm = pl.BlockSpec(memory_space=pl.ANY)
    V = pltpu.VMEM
    results = pl.pallas_call(
        kernel,
        out_shape=(
            jax.ShapeDtypeStruct((ROWS, OWN2), BF16),
            jax.ShapeDtypeStruct((KW1, BASES, OWN1), F32),
            jax.ShapeDtypeStruct((OWN1,), F32),
            jax.ShapeDtypeStruct((KW2, 6, OWN2), F32),
            jax.ShapeDtypeStruct((OWN2,), F32),
        ),
        in_specs=[hbm] * 6,
        out_specs=(vmem,) * 5,
        scratch_shapes=[
            V((ROWS,), jnp.int32),
            V((OWN1,), F32),
            V((OWN2,), F32),
            V((1, 640), jnp.int32),
            V((FRAME, OWN2), BF16),
            V((NC, KW1, BASES, OWN1), BF16),
            V((NC, 1, OWN1), F32),
            V((1, D1), F32),
            V((1, OWN2), F32),
            V((64, D1), BF16),
            V((64, 512), F32),
            V((512, 64), BF16),
            V((FRAME, D1), F32),
            V((FRAME, 128), F32),
            V((ROWS, D1), F32),
            V((FRAME, D1), BF16),
            V((D1, ROWS), F32),
            V((NX, SHARE, ROWS), BF16),
            V((NX, SHARE, ROWS), BF16),
            V((D1, WIDE), BF16),
            V((FRAME, WIDE), F32),
            V((FRAME, OWN2), F32),
            V((FRAME, OWN2), F32),
            V((512, 128), F32),
            V((512, 128), F32),
            V((512, 128), F32),
            V((NC, 1, 512), F32),
            V((NC, 1, 512), F32),
            V((2, FRAME, 128), F32),
            V((NX, 2, FRAME, 128), BF16),
            V((FRAME, 128), F32),
            V((NX * ROWS, WIDE), BF16),
            V((1, OWN2), F32),
            V((1, D1), F32),
            V((ROWS, D1), BF16),
            V((ROWS, D1), BF16),
            V((64, D1), F32),
            V((NC, 96, 128), BF16),
            V((NC, 96, 128), BF16),
            V((NX, 16, 256), BF16),
            V((NX, 16, 256), BF16),
            V((NY, 16, 256), BF16),
            V((NZ, 16, 256), BF16),
            V((NX, 16, 256), F32),
            V((SHARE, HALF), F32),
            V((NZ, NY, 16, 128), F32),
            V((2, NZ, NY, 16, 128), BF16),
            V((2, NZ, NY, 16, 128), BF16),
            V((2, NY, 16, 128), BF16),
            V((2, NY, 16, 128), BF16),
            V((2, NY, 80, 128), BF16),
            V((2, NY, 80, 128), BF16),
            V((80, 128), F32),
            V((NZ, 32, 128), F32),
            V((2, NZ, 32, 128), BF16),
            V((2, NZ, 32, 128), BF16),
            pltpu.SemaphoreType.DMA((N_SEM,)),
            pltpu.SemaphoreType.DMA((N_SEM,)),
            pltpu.SemaphoreType.DMA((15,)),
        ],
        compiler_params=pltpu.CompilerParams(
            collective_id=0, has_side_effects=True, vmem_limit_bytes=58 * 1024 * 1024
        ),
        cost_estimate=pl.CostEstimate(
            flops=3 * 2 * ROWS * D1 * KW2 * OWN2, bytes_accessed=4 << 20, transcendentals=1 << 20
        ),
    )(
        bases,
        conv1_weight.transpose(1, 0, 2),
        gain1,
        conv2_weight.transpose(1, 0, 2),
        gain2,
        cotangent,
    )
    features, gw1, gg1, gw2, gg2 = pl.pallas_call(
        write_out,
        out_shape=tuple(jax.ShapeDtypeStruct(r.shape, r.dtype) for r in results),
        in_specs=[vmem] * 5,
        out_specs=(hbm,) * 5,
        scratch_shapes=[pltpu.SemaphoreType.DMA((5,))],
    )(*results)
    return (features, gw1.transpose(1, 0, 2), gg1, gw2.transpose(1, 0, 2), gg2)


def solution(mesh):
    in_specs = (
        P("seq"),
        P(None, None, "ch"),
        P("ch"),
        P(None, None, "ch"),
        P("ch"),
        P("seq", "ch"),
    )
    out_specs = (P("seq", "ch"), P(None, None, "ch"), P("ch"), P("seq", None, "ch"), P("ch"))
    return jax.shard_map(
        on_device, mesh=mesh, in_specs=in_specs, out_specs=out_specs, check_vma=False
    )
```

```python
import math

import jax
import jax.numpy as jnp
from jax import lax
from jax.experimental import pallas as pl
from jax.experimental.pallas import tpu as pltpu
from jax.sharding import PartitionSpec as P

BASES = 4
KW1 = 15
KW2 = 5
D1 = 768
D2 = 1024
OWN1 = 192
OWN2 = 256
ROWS = 384
FRAME = 416
NX, NY, NZ, NC = 4, 8, 4, 4
NS = NX * NY * NZ
TAPS1 = KW1 * BASES
WIDE = KW2 * OWN2
HALF = WIDE // 2
SHARE = D1 // NX
EPS = 1e-06
MESH = pl.DeviceIdType.MESH
F32 = jnp.float32
BF16 = jnp.bfloat16
ROOT = math.sqrt(2.0 / math.pi)

S_BASE, S_COT, S_W1, S_G1 = 0, 2, 4, 7
S_SQ, S_IN, S_CH = 10, 13, 16
S_ACT, S_D2 = 19, 22
S_RX, S_RY, S_RZ, S_RG = 28, 31, 38, 41
S_Y1, S_Z1, S_Z2, S_Y2 = 44, 58, 64, 70
N_SEM = 84


def gelu_parts(v):
    square = v * v
    t = jnp.tanh(ROOT * (v + 0.044715 * (square * v)))
    cdf = 0.5 * (1.0 + t)
    slope = cdf + (0.5 * ROOT) * v * (1.0 - t * t) * (1.0 + (3.0 * 0.044715) * square)
    return cdf, slope


def nt_dot(a, b):
    return lax.dot_general(a, b, (((1,), (1,)), ((), ())), preferred_element_type=F32)


def tn_dot(a, b):
    return lax.dot_general(a, b, (((0,), (0,)), ((), ())), preferred_element_type=F32)


def kernel(
    bases_hbm, w1_hbm, g1_hbm, w2_ref, g2_hbm, cot_ref,
    feat_ref, gw1_ref, gg1_ref, gw2_ref, gg2_ref,
    bases_ref, g1_ref, g2_ref, bext, cext, w1g, g1g, gain1, gain2, w1full, ut, uu, n1, s1, h1, act, actt, asel, aget,
    w2v, ybuf, c2, dn2, q, s2, m2, sqs, ins, d2, d2s, d2f, dcat, g2acc, g1acc,
    dact, dc1, pay, chs, chr_, rsend, rxs, rys, rzs, rgs,
    part, zpack, zbig, rz0, yb, ry0, big, ryg, fin, zfin, zsl, rzl,
    ssem, rsem, lsem,
):
    s = lax.axis_index("seq")
    c = lax.axis_index("ch")
    z = lax.rem(s, NZ)
    x = lax.rem(lax.div(s, NZ), NX)
    y = lax.div(s, NZ * NX)

    def seq_of(yy, xx, zz):
        return (yy * NX + xx) * NZ + zz

    def x_peer(k):
        return lax.rem(x + k, NX)

    def y_peer(k):
        return lax.rem(y + k, NY)

    def z_peer(k):
        return lax.rem(z + k, NZ)

    def c_peer(k):
        return lax.rem(c + k, NC)

    right = lax.rem(s + 1, NS)
    left = lax.rem(s + NS - 1, NS)

    first_loads = [
        pltpu.make_async_copy(bases_hbm, bases_ref, lsem.at[11]),
        pltpu.make_async_copy(w1_hbm, w1g.at[c], lsem.at[12]),
        pltpu.make_async_copy(g1_hbm, g1_ref, lsem.at[13]),
        pltpu.make_async_copy(g2_hbm, g2_ref, lsem.at[14]),
    ]
    for load in first_loads:
        load.start()
    loads = []
    for half in range(2):
        for tap in range(KW2):
            n = half * KW2 + tap
            loads.append(
                pltpu.make_async_copy(
                    w2_ref.at[tap, :, pl.ds(128 * half, 128)],
                    w2v.at[:, pl.ds(128 * n, 128)],
                    lsem.at[n],
                )
            )
    for load in loads:
        load.start()
    load_cot = pltpu.make_async_copy(cot_ref, cext.at[pl.ds(16, ROWS)], lsem.at[10])
    load_cot.start()

    barrier = pltpu.get_barrier_semaphore()
    friends = [(right, c), (left, c)]
    friends += [(s, c_peer(k)) for k in range(1, NC)]
    friends += [(seq_of(y, x_peer(k), z), c) for k in range(1, NX)]
    friends += [(seq_of(y_peer(k), x, z), c) for k in range(1, NY)]
    friends += [(seq_of(y, x, z_peer(k)), c) for k in range(1, NZ)]
    for friend in friends:
        pl.semaphore_signal(barrier, inc=1, device_id=friend, device_id_type=MESH)
    for load in first_loads:
        load.wait()
    bext[:, pl.ds(128, ROWS)] = bases_ref[...].reshape(1, ROWS)
    g1g[c] = g1_ref[...].reshape(1, OWN1)
    gain2[...] = g2_ref[...].reshape(1, OWN2)
    pl.semaphore_wait(barrier, len(friends))

    pending = []

    def send(src, dst, number, to):
        copy = pltpu.make_async_remote_copy(
            src_ref=src,
            dst_ref=dst,
            send_sem=ssem.at[number],
            recv_sem=rsem.at[number],
            device_id=to,
            device_id_type=MESH,
        )
        copy.start()
        pending.append(copy)
        return copy

    def arrived(copies):
        for copy in copies:
            copy.wait_recv()

    got_bases = [
        send(bext.at[:, pl.ds(384, 128)], bext.at[:, pl.ds(0, 128)], S_BASE, (right, c)),
        send(bext.at[:, pl.ds(128, 128)], bext.at[:, pl.ds(512, 128)], S_BASE + 1, (left, c)),
    ]
    got_w1 = []
    for k in (2, 1, 3):
        to = (s, c_peer(k))
        got_w1.append(send(w1g.at[c], w1g.at[c], S_W1 + k - 1, to))
        got_w1.append(send(g1g.at[c], g1g.at[c], S_G1 + k - 1, to))
    got_cot = [
        send(cot_ref.at[pl.ds(ROWS - 16, 16)], cext.at[pl.ds(0, 16)], S_COT, (right, c)),
        send(cot_ref.at[pl.ds(0, 16)], cext.at[pl.ds(16 + ROWS, 16)], S_COT + 1, (left, c)),
    ]

    arrived(got_bases)
    place = lax.broadcasted_iota(jnp.int32, (1, 640), 1) - 128 + s * ROWS
    known = jnp.where((place >= 0) & (place < NS * ROWS), bext[...], -1)
    kinds = lax.broadcasted_iota(jnp.int32, (BASES, 512), 0)
    for tap in range(KW1):
        rolled = pltpu.roll(known, 640 - (105 + tap), 1)[:, :512]
        ut[pl.ds(BASES * tap, BASES), :] = (
            jnp.broadcast_to(rolled, (BASES, 512)) == kinds
        ).astype(F32)
    ut[pl.ds(BASES * KW1, 4), :] = jnp.zeros((4, 512), F32)
    for block in range(4):
        uu[pl.ds(128 * block, 128), :] = ut[:, pl.ds(128 * block, 128)].T.astype(BF16)

    arrived(got_w1)
    w1full[pl.ds(0, TAPS1), :] = jnp.concatenate(
        [w1g[k].astype(F32).reshape(TAPS1, OWN1) for k in range(NC)], axis=1
    ).astype(BF16)
    w1full[pl.ds(TAPS1, 4), :] = jnp.zeros((4, D1), BF16)
    gain1[...] = jnp.concatenate([g1g[k] for k in range(NC)], axis=1)
    n1[...] = jnp.dot(uu[pl.ds(0, FRAME), :], w1full[...], preferred_element_type=F32)

    @pl.loop(0, FRAME // 32)
    def _(i):
        rows = pl.ds(pl.multiple_of(i * 32, 32), 32)
        v = n1[rows, :]
        scale = lax.rsqrt(jnp.sum(v * v, axis=1, keepdims=True) * (1.0 / D1) + EPS)
        normed = v * scale
        n1[rows, :] = normed
        s1[rows, :] = jnp.broadcast_to(scale, (32, 128))
        pre = normed * gain1[...]
        cdf, _ = gelu_parts(pre)
        where = lax.broadcasted_iota(jnp.int32, (32, 1), 0) + (i * 32 - 16) + s * ROWS
        inside = (where >= 0) & (where < NS * ROWS)
        act[rows, :] = jnp.where(inside, pre * cdf, 0.0).astype(BF16)

    for load in loads:
        load.wait()
    ybuf[...] = jnp.dot(act[...], w2v[...], preferred_element_type=F32)
    pieces = [(8, 8)] + [(16 + 48 * k, 48) for k in range(8)] + [(400, 8)]
    q[pl.ds(0, 8), :] = jnp.zeros((8, 128), F32)
    q[pl.ds(408, 104), :] = jnp.zeros((104, 128), F32)
    for start, count in pieces:
        squares = None
        for half in range(2):
            total = None
            for tap in range(KW2):
                term = ybuf[
                    pl.ds(start + tap - 2, count), pl.ds(128 * (half * KW2 + tap), 128)
                ]
                total = term if total is None else total + term
            c2[pl.ds(start, count), pl.ds(128 * half, 128)] = total
            squares = total * total if squares is None else squares + total * total
        q[pl.ds(start, count), :] = squares
    def row_sums(slots, number):
        for block in range(4):
            slots[c, :, pl.ds(128 * block, 128)] = jnp.sum(
                q[pl.ds(128 * block, 128), :].T, axis=0, keepdims=True
            )
        return [
            send(slots.at[c], slots.at[c], number + k - 1, (s, c_peer(k))) for k in (2, 1, 3)
        ]

    def spread(row, columns):
        for block in range(4):
            columns[pl.ds(128 * block, 128), :] = jnp.broadcast_to(
                row[:, 128 * block : 128 * block + 128], (128, 128)
            ).T

    got_sq = row_sums(sqs, S_SQ)
    for a in range(3):
        for b in range(6):
            tile = act[pl.ds(16 + 128 * a, 128), pl.ds(128 * b, 128)].astype(F32)
            actt[pl.ds(128 * b, 128), pl.ds(128 * a, 128)] = tile.T
    for xx in range(NX):
        for yy in range(0, NY, 2):
            asel[xx, pl.ds(24 * yy, 48), :] = jnp.concatenate(
                [
                    actt[pl.ds(96 * yy + 24 * xx, 24), :],
                    actt[pl.ds(96 * yy + 96 + 24 * xx, 24), :],
                ],
                axis=0,
            ).astype(BF16)
    got_act = [
        send(asel.at[x_peer(k)], aget.at[x], S_ACT + k - 1, (seq_of(y, x_peer(k), z), c))
        for k in range(1, NX)
    ]
    aget[x] = asel[x]

    @pl.loop(0, ROWS // 32)
    def _(i):
        local = pl.ds(pl.multiple_of(i * 32, 32), 32)
        gain = gain1[...]
        _, slope = gelu_parts(n1[pl.ds(pl.multiple_of(i * 32 + 16, 16), 32), :] * gain)
        h1[local, :] = slope * gain

    load_cot.wait()
    arrived(got_cot)
    arrived(got_sq)
    spread(
        lax.rsqrt((sqs[0] + sqs[1] + sqs[2] + sqs[3]) * (1.0 / D2) + EPS), s2
    )
    g2acc[...] = jnp.zeros_like(g2acc)

    def second_norm(rows, cot, own, count):
        scale = s2[rows, :]
        scale = jnp.concatenate([scale, scale], axis=1)
        normed = c2[rows, :] * scale
        gain = gain2[...]
        pre = normed * gain
        cdf, slope = gelu_parts(pre)
        dpre = cot * slope
        dnormed = dpre * gain
        inner = dnormed * normed
        c2[rows, :] = normed
        dn2[rows, :] = dnormed
        q[rows, :] = inner[:, :128] + inner[:, 128:]
        if own is not None:
            feat_ref[own, :] = (pre * cdf).astype(BF16)
            g2acc[...] += jnp.sum(dpre * normed, axis=0, keepdims=True)

    second_norm(pl.ds(8, 8), cext[pl.ds(0, 16), :].astype(F32)[8:16], None, 8)
    second_norm(pl.ds(400, 8), cext[pl.ds(400, 16), :].astype(F32)[0:8], None, 8)

    @pl.loop(0, 8)
    def _(i):
        rows = pl.ds(pl.multiple_of(16 + i * 48, 16), 48)
        own = pl.ds(pl.multiple_of(i * 48, 16), 48)
        second_norm(rows, cext[rows, :].astype(F32), own, 48)

    got_in = row_sums(ins, S_IN)
    arrived(got_in)
    spread((ins[0] + ins[1] + ins[2] + ins[3]) * (1.0 / D2), m2)

    def rows_of(b):
        return pl.ds(pl.multiple_of(b * ROWS, 128), ROWS)

    def expand(b, half):
        for tap in range(KW2):
            for k in range(8):
                dcat[
                    pl.ds(pl.multiple_of(b * ROWS + 48 * k, 16), 48),
                    pl.ds(128 * (half * KW2 + tap), 128),
                ] = d2f[pl.ds(48 * k + 18 - tap, 48), :].astype(BF16)

    got_d2 = []
    for half in range(2):
        columns = pl.ds(128 * half, 128)
        d2[half, pl.ds(0, 8), :] = jnp.zeros((8, 128), F32)
        d2[half, pl.ds(408, 8), :] = jnp.zeros((8, 128), F32)
        for start, count in pieces:
            rows = pl.ds(start, count)
            grad = s2[rows, :] * (dn2[rows, columns] - c2[rows, columns] * m2[rows, :])
            if start == 8:
                grad = jnp.where(s > 0, grad, 0.0)
            if start == 400:
                grad = jnp.where(s < NS - 1, grad, 0.0)
            d2[half, rows, :] = grad
        d2s[x, half] = d2[half].astype(BF16)
        got_d2.append(
            [
                send(
                    d2s.at[x, half],
                    d2s.at[x, half],
                    S_D2 + 3 * half + k - 1,
                    (seq_of(y, x_peer(k), z), c),
                )
                for k in range(1, NX)
            ]
        )
    for half in range(2):
        d2f[...] = d2[half]
        expand(x, half)
    dact[...] = nt_dot(dcat[rows_of(x), :], w2v[...]).astype(BF16)
    g1acc[...] = jnp.zeros_like(g1acc)

    @pl.loop(0, ROWS // 32)
    def _(i):
        local = pl.ds(pl.multiple_of(i * 32, 32), 32)
        rows = pl.ds(pl.multiple_of(16 + i * 32, 16), 32)
        normed = n1[rows, :]
        dnormed = dact[local, :].astype(F32) * h1[local, :]
        inner = dnormed * normed
        g1acc[...] += jnp.sum(inner, axis=0, keepdims=True)
        mean = jnp.sum(inner, axis=1, keepdims=True) * (1.0 / D1)
        dc1[local, :] = (s1[rows, :][:, :1] * (dnormed - normed * mean)).astype(BF16)

    pay[...] = tn_dot(uu[pl.ds(16, ROWS), :], dc1[...])
    pay[pl.ds(60, 1), :] = g1acc[...] / gain1[...]
    for k in range(NC):
        chs[k, pl.ds(0, 64), :] = pay[:, OWN1 * k : OWN1 * k + 128].astype(BF16)
        rest = pay[:, OWN1 * k + 128 : OWN1 * k + 192]
        chs[k, pl.ds(64, 32), :] = jnp.concatenate([rest[:32], rest[32:]], axis=1).astype(BF16)
    got_ch = [
        send(chs.at[c_peer(k)], chr_.at[c], S_CH + k - 1, (s, c_peer(k))) for k in (2, 1, 3)
    ]
    chr_[c] = chs[c]

    def add_up(slots, count):
        total = slots[0].astype(F32)
        for k in range(1, count):
            total = total + slots[k].astype(F32)
        return total

    def half_grad(half):
        arrived(got_d2[half])
        for k in range(1, NX):
            b = x_peer(k)
            d2f[...] = d2s[b, half].astype(F32)
            expand(b, half)
        columns = pl.ds(HALF * half, HALF)
        total = jnp.dot(aget[0], dcat[pl.ds(0, ROWS), columns], preferred_element_type=F32)
        for b in range(1, NX):
            total = total + jnp.dot(
                aget[b], dcat[pl.ds(ROWS * b, ROWS), columns], preferred_element_type=F32
            )
        part[...] = total

    def pack(half):
        for yy in range(NY):
            rows = pl.ds(24 * yy, 24)
            taps = [part[rows, pl.ds(128 * tap, 128)] for tap in range(3)]
            big[half, yy, pl.ds(0, 48), :] = jnp.concatenate(taps[:2], axis=0).astype(BF16)
            big[half, yy, pl.ds(48, 32), :] = jnp.concatenate(
                [taps[2], jnp.zeros((8, 128), F32)], axis=0
            ).astype(BF16)
            for zz in range(NZ):
                for tap in (3, 4):
                    zpack[zz, yy, pl.ds(6 * tap - 18, 6), :] = part[
                        pl.ds(24 * yy + 6 * zz, 6), pl.ds(128 * tap, 128)
                    ]
        zpack[:, :, pl.ds(12, 4), :] = jnp.zeros((NZ, NY, 4, 128), F32)
        zbig[half] = zpack[...].astype(BF16)

    def y_sends(blocks, slots, half, number):
        copies = [
            send(
                blocks.at[half, y_peer(k)],
                slots.at[half, y],
                number + 7 * half + k - 1,
                (seq_of(y_peer(k), x, z), c),
            )
            for k in (4, 3, 5, 2, 6, 1, 7)
        ]
        slots[half, y] = blocks[half, y]
        return copies

    def z_sends(blocks, slots, half, number):
        copies = [
            send(
                blocks.at[half, z_peer(k)],
                slots.at[half, z],
                number + 3 * half + k - 1,
                (seq_of(y, x, z_peer(k)), c),
            )
            for k in (2, 1, 3)
        ]
        slots[half, z] = blocks[half, z]
        return copies

    def add_half(slots, half, count):
        total = slots[half, 0].astype(F32)
        for k in range(1, count):
            total = total + slots[half, k].astype(F32)
        return total

    def first_stage(half):
        return y_sends(big, ryg, half, S_Y1), z_sends(zbig, rz0, half, S_Z1)

    def second_stage(half, got):
        arrived(got[1])
        yb[half] = add_half(rz0, half, NZ).astype(BF16)
        over_y = y_sends(yb, ry0, half, S_Y2)
        arrived(got[0])
        fin[...] = add_half(ryg, half, NY)
        for zz in range(NZ):
            for tap in range(3):
                zfin[zz, pl.ds(6 * tap, 6), :] = fin[pl.ds(24 * tap + 6 * zz, 6), :]
            zfin[zz, pl.ds(18, 14), :] = jnp.zeros((14, 128), F32)
        zsl[half] = zfin[...].astype(BF16)
        return over_y, z_sends(zsl, rzl, half, S_Z2)

    def last_stage(half, got):
        columns = pl.ds(128 * half, 128)
        arrived(got[0])
        total = add_half(ry0, half, NY)
        for tap in (3, 4):
            gw2_ref[tap, :, columns] = total[6 * tap - 18 : 6 * tap - 12]
        arrived(got[1])
        total = add_half(rzl, half, NZ)
        for tap in range(3):
            gw2_ref[tap, :, columns] = total[6 * tap : 6 * tap + 6]

    arrived(got_act)
    half_grad(0)
    pack(0)
    first0 = first_stage(0)
    arrived(got_ch)
    small = add_up(chr_, NC)
    rest = small[64:]
    pay[:, pl.ds(0, 128)] = small[:64]
    pay[pl.ds(0, 32), pl.ds(128, 128)] = rest
    pay[pl.ds(32, 32), pl.ds(128, 128)] = jnp.concatenate([rest[:, 64:], rest[:, :64]], axis=1)
    pay[pl.ds(61, 1), pl.ds(0, 128)] = g2acc[:, :128]
    pay[pl.ds(62, 1), pl.ds(0, 128)] = g2acc[:, 128:]
    for k in range(NX):
        rsend[k] = pay[pl.ds(16 * k, 16), pl.ds(0, 256)].astype(BF16)
    got_rx = [
        send(rsend.at[x_peer(k)], rxs.at[x], S_RX + k - 1, (seq_of(y, x_peer(k), z), c))
        for k in range(1, NX)
    ]
    rxs[x] = rsend[x]
    arrived(got_rx)
    rys[y] = add_up(rxs, NX).astype(BF16)
    got_ry = [
        send(rys.at[y], rys.at[y], S_RY + k - 1, (seq_of(y_peer(k), x, z), c))
        for k in (4, 3, 5, 2, 6, 1, 7)
    ]
    half_grad(1)
    pack(1)
    first1 = first_stage(1)
    second0 = second_stage(0, first0)
    arrived(got_ry)
    rzs[z] = add_up(rys, NY).astype(BF16)
    got_rz = [
        send(rzs.at[z], rzs.at[z], S_RZ + k - 1, (seq_of(y, x, z_peer(k)), c)) for k in range(1, NZ)
    ]
    second1 = second_stage(1, first1)
    arrived(got_rz)
    rgs[x] = add_up(rzs, NZ)
    got_rg = [
        send(rgs.at[x], rgs.at[x], S_RG + k - 1, (seq_of(y, x_peer(k), z), c)) for k in range(1, NX)
    ]
    last_stage(0, second0)
    last_stage(1, second1)
    arrived(got_rg)
    for k in range(NX):
        for j in range(4):
            tap = 4 * k + j
            if tap < KW1:
                gw1_ref[tap] = rgs[k, pl.ds(4 * j, 4), pl.ds(0, OWN1)]
    gg1_ref[...] = rgs[3, pl.ds(12, 1), pl.ds(0, OWN1)].reshape(OWN1)
    gg2_ref[...] = jnp.concatenate(
        [rgs[3, pl.ds(13, 1), pl.ds(0, 128)], rgs[3, pl.ds(14, 1), pl.ds(0, 128)]], axis=1
    ).reshape(OWN2)
    for copy in pending:
        copy.wait_send()


def write_out(*refs):
    copies = [pltpu.make_async_copy(refs[i], refs[5 + i], refs[10].at[i]) for i in range(5)]
    for copy in copies:
        copy.start()
    for copy in copies:
        copy.wait()


def on_device(bases, conv1_weight, gain1, conv2_weight, gain2, cotangent):
    vmem = pl.BlockSpec(memory_space=pltpu.VMEM)
    hbm = pl.BlockSpec(memory_space=pl.ANY)
    V = pltpu.VMEM
    results = pl.pallas_call(
        kernel,
        out_shape=(
            jax.ShapeDtypeStruct((ROWS, OWN2), BF16),
            jax.ShapeDtypeStruct((KW1, BASES, OWN1), F32),
            jax.ShapeDtypeStruct((OWN1,), F32),
            jax.ShapeDtypeStruct((KW2, 6, OWN2), F32),
            jax.ShapeDtypeStruct((OWN2,), F32),
        ),
        in_specs=[hbm] * 6,
        out_specs=(vmem,) * 5,
        scratch_shapes=[
            V((ROWS,), jnp.int32),
            V((OWN1,), F32),
            V((OWN2,), F32),
            V((1, 640), jnp.int32),
            V((FRAME, OWN2), BF16),
            V((NC, KW1, BASES, OWN1), BF16),
            V((NC, 1, OWN1), F32),
            V((1, D1), F32),
            V((1, OWN2), F32),
            V((64, D1), BF16),
            V((64, 512), F32),
            V((512, 64), BF16),
            V((FRAME, D1), F32),
            V((FRAME, 128), F32),
            V((ROWS, D1), F32),
            V((FRAME, D1), BF16),
            V((D1, ROWS), F32),
            V((NX, SHARE, ROWS), BF16),
            V((NX, SHARE, ROWS), BF16),
            V((D1, WIDE), BF16),
            V((FRAME, WIDE), F32),
            V((FRAME, OWN2), F32),
            V((FRAME, OWN2), F32),
            V((512, 128), F32),
            V((512, 128), F32),
            V((512, 128), F32),
            V((NC, 1, 512), F32),
            V((NC, 1, 512), F32),
            V((2, FRAME, 128), F32),
            V((NX, 2, FRAME, 128), BF16),
            V((FRAME, 128), F32),
            V((NX * ROWS, WIDE), BF16),
            V((1, OWN2), F32),
            V((1, D1), F32),
            V((ROWS, D1), BF16),
            V((ROWS, D1), BF16),
            V((64, D1), F32),
            V((NC, 96, 128), BF16),
            V((NC, 96, 128), BF16),
            V((NX, 16, 256), BF16),
            V((NX, 16, 256), BF16),
            V((NY, 16, 256), BF16),
            V((NZ, 16, 256), BF16),
            V((NX, 16, 256), F32),
            V((SHARE, HALF), F32),
            V((NZ, NY, 16, 128), F32),
            V((2, NZ, NY, 16, 128), BF16),
            V((2, NZ, NY, 16, 128), BF16),
            V((2, NY, 16, 128), BF16),
            V((2, NY, 16, 128), BF16),
            V((2, NY, 80, 128), BF16),
            V((2, NY, 80, 128), BF16),
            V((80, 128), F32),
            V((NZ, 32, 128), F32),
            V((2, NZ, 32, 128), BF16),
            V((2, NZ, 32, 128), BF16),
            pltpu.SemaphoreType.DMA((N_SEM,)),
            pltpu.SemaphoreType.DMA((N_SEM,)),
            pltpu.SemaphoreType.DMA((15,)),
        ],
        compiler_params=pltpu.CompilerParams(
            collective_id=0, has_side_effects=True, vmem_limit_bytes=58 * 1024 * 1024
        ),
        cost_estimate=pl.CostEstimate(
            flops=3 * 2 * ROWS * D1 * KW2 * OWN2, bytes_accessed=4 << 20, transcendentals=1 << 20
        ),
    )(
        bases,
        conv1_weight.transpose(1, 0, 2),
        gain1,
        conv2_weight.transpose(1, 0, 2),
        gain2,
        cotangent,
    )
    features, gw1, gg1, gw2, gg2 = pl.pallas_call(
        write_out,
        out_shape=tuple(jax.ShapeDtypeStruct(r.shape, r.dtype) for r in results),
        in_specs=[vmem] * 5,
        out_specs=(hbm,) * 5,
        scratch_shapes=[pltpu.SemaphoreType.DMA((5,))],
    )(*results)
    return (features, gw1.transpose(1, 0, 2), gg1, gw2.transpose(1, 0, 2), gg2)


def solution(mesh):
    in_specs = (
        P("seq"),
        P(None, None, "ch"),
        P("ch"),
        P(None, None, "ch"),
        P("ch"),
        P("seq", "ch"),
    )
    out_specs = (P("seq", "ch"), P(None, None, "ch"), P("ch"), P("seq", None, "ch"), P("ch"))
    return jax.shard_map(
        on_device, mesh=mesh, in_specs=in_specs, out_specs=out_specs, check_vma=False
    )
```
